512 devices in a mesh: branch: 64 (over y_hi, z, core), tensor: 8 (over y_lo, x).
Axes of the slice: x: 4, y: 4 (y_hi: 2, y_lo: 2; y = y_hi * 2 + y_lo), z: 16, core: 2. Of those that a mesh axis runs over, the one named last changes fastest.
Arguments:
- prefix_hidden: bfloat16 [4096, 8192], P('branch', 'tensor'), may hold values from -6 to 6
- key_weight: bfloat16 [8192, 1024], P('branch', 'tensor'), may hold values from -0.0625 to 0.0625
- value_weight: bfloat16 [8192, 1024], P('branch', 'tensor'), may hold values from -0.0625 to 0.0625
- suffix_q: bfloat16 [16384, 8192], P('branch', 'tensor'), may hold values from -35 to 35
- suffix_k: bfloat16 [16384, 1024], P('branch', 'tensor'), may hold values from -6 to 6
- suffix_v: bfloat16 [16384, 1024], P('branch', 'tensor'), may hold values from -6 to 6
- slab_node: int32 [64], replicated, may hold values from 0 to 11, as said below
- slab_len: int32 [64], replicated, may hold values from 1 to 64, as said below
- parent: int32 [12], replicated, may hold values from 0 to 10, as said below
- leaf: int32 [64], P('branch'), may hold values from 0 to 11
- suffix_len: int32 [64], P('branch'), may hold values from 128 to 256, as said below
Outputs:
- attended: bfloat16 [16384, 8192], P('branch', 'tensor')
The draws below stay inside these ranges and needn't reach their ends.
Inputs may be any that keep to these rules, and one draw needn't show every extreme that they name: `slab_node`: Non-decreasing along slabs; every node holds one or more consecutive slabs. `slab_len`: every slab except the last slab of its node is full. parent[0] = 0, parent[n] < n for n >= 1, and the last node's parent is the node just before it. `suffix_len`: some group is full.
All inputs are finite; a program needn't handle non-finite values.
Results may differ from the reference program's by a relative error of at most 0.0075.
Values may be sent and summed in bfloat16 or wider, within the bound.
A program may use at most 64 MiB of HBM per device.

```python
import math
import jax
import jax.numpy as jnp
from jax import lax

D = 8192
HEADS = 64
KV_HEADS = 8
HEAD = 128
NODES = 12
SLAB = 64
SUF = 256
KVW = 1024
PREF = 4096
ROWS = 16384
N_BRANCH = 64


def shared_keys(key):
    normal_part = jnp.clip(jax.random.normal(jax.random.fold_in(key, 11), (N_BRANCH * SUF, KV_HEADS * HEAD), jnp.float32), -6.0, 6.0)
    return normal_part


def slab_cuts(key):
    order = jax.random.permutation(jax.random.fold_in(key, 21), N_BRANCH - 1) + 1
    return jnp.sort(order[:NODES - 1]).astype(jnp.int32)


def draw_suffix_k(key, part):
    shared = shared_keys(key)
    return shared.astype(jnp.bfloat16)


def draw_suffix_q(key, part):
    key = jax.random.fold_in(key, 5)
    fresh = jnp.clip(jax.random.normal(key, (N_BRANCH * SUF, HEADS * HEAD), jnp.float32), -6.0, 6.0)
    return fresh.astype(jnp.bfloat16)


def draw_slab_node(key, part):
    cuts = slab_cuts(key)
    slab_ids = jnp.arange(N_BRANCH, dtype=jnp.int32)
    return jnp.sum((slab_ids[:, None] >= cuts[None, :]).astype(jnp.int32), axis=1).astype(jnp.int32)


def draw_slab_len(key, part):
    cuts = slab_cuts(key)
    key = jax.random.fold_in(key, 8)
    slab_ids = jnp.arange(N_BRANCH, dtype=jnp.int32)
    closing = jnp.any(cuts[None, :] == slab_ids[:, None] + 1, axis=1) | (slab_ids == N_BRANCH - 1)
    ragged = jax.random.randint(key, (N_BRANCH,), 1, SLAB + 1)
    return jnp.where(closing, ragged, SLAB).astype(jnp.int32)


def draw_parent(key, part):
    key = jax.random.fold_in(key, 9)
    node_ids = jnp.arange(NODES, dtype=jnp.int32)
    drawn = jax.random.randint(key, (NODES,), 0, jnp.maximum(node_ids, 1)).astype(jnp.int32)
    return jnp.where(node_ids == NODES - 1, NODES - 2, drawn).astype(jnp.int32)


def draw_suffix_len(key, part):
    key = jax.random.fold_in(key, 10)
    lengths = jax.random.randint(jax.random.fold_in(key, 1), (N_BRANCH,), SUF // 2, SUF + 1)
    filled = jax.random.randint(jax.random.fold_in(key, 2), (), 0, N_BRANCH)
    return jnp.where(jnp.arange(N_BRANCH, dtype=jnp.int32) == filled, SUF, lengths).astype(jnp.int32)


def with_ends(values, rng, low, top_value):
    dims = values.shape
    spot = [jax.random.randint(jax.random.fold_in(rng, axis), (), 0, dims[axis]) for axis in range(len(dims))]
    values = values.at[tuple(spot)].set(low)
    longest = dims.index(max(dims))
    spot[longest] = (spot[longest] + 1) % dims[longest]
    return values.at[tuple(spot)].set(top_value)


def shard_levels(stream_key, shape, cuts, least, high):
    level = 1.0
    for position, parts in cuts:
        steps = jax.random.uniform(jax.random.fold_in(jax.random.fold_in(stream_key, 6), position), (parts,), jnp.float32, least / len(cuts), high / len(cuts))
        level = level * jnp.repeat(jnp.exp(steps), shape[position] // parts).reshape((-1,) + (1,) * (len(shape) - 1 - position))
    return level


def gaussian(own_key, dims, width, reach, pieces=(), kind=jnp.bfloat16):
    result = jax.random.normal(own_key, dims, jnp.float32) * width
    if len(pieces) > 0:
        result = shard_levels(own_key, dims, pieces, -0.22, 0.18) * result
    return jnp.clip(result, min=-reach, max=reach).astype(kind)


def setup_inputs(seed: int = 0) -> dict:
    seeds = jax.random.split(jax.random.key(seed), 12)
    prefix_hidden = gaussian(seeds[0], (PREF, D), 1.0, 6.0, ((0, 64), (1, 8)))
    key_weight = gaussian(seeds[1], (D, KVW), D ** -0.5, 0.0625, ((0, 64), (1, 8)))
    value_weight = gaussian(seeds[2], (D, KVW), D ** -0.5, 0.0625, ((0, 64), (1, 8)))
    suffix_q = draw_suffix_q(jax.random.fold_in(seeds[11], 71), 0)
    suffix_k = draw_suffix_k(jax.random.fold_in(seeds[11], 71), 0)
    suffix_v = gaussian(seeds[5], (ROWS, KVW), 1.0, 6.0, ((0, 64), (1, 8)))
    slab_node = draw_slab_node(jax.random.fold_in(seeds[11], 71), 0)
    slab_len = draw_slab_len(jax.random.fold_in(seeds[11], 71), 0)
    parent = draw_parent(jax.random.fold_in(seeds[11], 71), 0)
    leaf = with_ends(jax.random.randint(seeds[9], (N_BRANCH,), 0, NODES), jax.random.fold_in(seeds[9], 1), 0, NODES - 1).astype(jnp.int32)
    suffix_len = draw_suffix_len(jax.random.fold_in(seeds[11], 71), 0)
    return dict(prefix_hidden=prefix_hidden, key_weight=key_weight, value_weight=value_weight, suffix_q=suffix_q, suffix_k=suffix_k, suffix_v=suffix_v, slab_node=slab_node, slab_len=slab_len, parent=parent, leaf=leaf, suffix_len=suffix_len)


rope_base = 500000.0
masked_score = -1e+30

def slab_bases(slab_node, slab_len, parent):
    node_count = parent.shape[0]
    node_ids = jnp.arange(node_count, dtype=jnp.int32)
    member = (slab_node[:, None] == node_ids[None, :]).astype(jnp.int32)
    node_length = lax.optimization_barrier(jnp.sum(member * slab_len[:, None], axis=0)).astype(jnp.int32)
    before = (jnp.cumsum(slab_len).astype(jnp.int32) - slab_len).astype(jnp.int32)
    node_first = lax.optimization_barrier(jnp.min(jnp.where(member > 0, before[:, None], 2 ** 30), axis=0)).astype(jnp.int32)
    node_start = jnp.zeros((node_count,), jnp.int32)
    for number in range(1, node_count):
        upper = jnp.sum(jnp.where(node_ids == parent[number], node_start + node_length, 0)).astype(jnp.int32)
        node_start = jnp.where(node_ids == number, upper, node_start).astype(jnp.int32)
    shift_node = (node_start - node_first).astype(jnp.int32)
    return (before + lax.optimization_barrier(jnp.sum(member * shift_node[None, :], axis=1))).astype(jnp.int32)

def path_nodes(leaf_node, parent):
    node_ids = jnp.arange(parent.shape[0], dtype=jnp.int32)
    current = leaf_node
    member = (node_ids == current).astype(jnp.int32)
    for unused in range(parent.shape[0]):
        current = jnp.sum(jnp.where(node_ids == current, parent, 0)).astype(jnp.int32)
        member = jnp.maximum(member, (node_ids == current).astype(jnp.int32))
    return member

def rotate(raw, positions, head_size):
    half_size = head_size // 2
    freqs = rope_base ** (-2.0 * jnp.arange(half_size, dtype=jnp.float32) / head_size)
    angles = positions.astype(jnp.float32)[:, None] * freqs[None, :]
    cosine = jnp.cos(angles)[:, None, :]
    sine = jnp.sin(angles)[:, None, :]
    shaped = raw.reshape(raw.shape[0], -1, head_size)
    first = shaped[..., :half_size]
    second = shaped[..., half_size:]
    turned = jnp.concatenate([first * cosine - second * sine, second * cosine + first * sine], axis=-1)
    return turned.reshape(raw.shape)

def reference(prefix_hidden, key_weight, value_weight, suffix_q, suffix_k, suffix_v, slab_node, slab_len, parent, leaf, suffix_len):
    bases = slab_bases(slab_node, slab_len, parent)
    row_ids = jnp.arange(PREF, dtype=jnp.int32)
    slab_of = (row_ids // SLAB).astype(jnp.int32)
    within = (row_ids % SLAB).astype(jnp.int32)
    positions = (bases[slab_of] + within).astype(jnp.int32)
    keys_raw = jnp.dot(prefix_hidden, key_weight, preferred_element_type=jnp.float32)
    prefix_key = rotate(keys_raw, positions, HEAD).astype(jnp.bfloat16)
    prefix_value = jnp.dot(prefix_hidden, value_weight, preferred_element_type=jnp.float32).astype(jnp.bfloat16)
    row_live = within < slab_len[slab_of]
    row_node = slab_node[slab_of]
    group_size = HEADS // KV_HEADS
    scale = 1.0 / math.sqrt(HEAD)
    prefix_key_heads = prefix_key.reshape(PREF, KV_HEADS, HEAD).transpose(1, 0, 2)
    prefix_value_heads = prefix_value.reshape(PREF, KV_HEADS, HEAD).transpose(1, 0, 2)
    query_pos = jnp.arange(SUF, dtype=jnp.int32)

    def one_group(inputs):
        queries, keys, values, leaf_node, length = inputs
        on_path = path_nodes(leaf_node, parent)
        prefix_mask = row_live & (on_path[row_node] > 0)
        suffix_mask = (query_pos[None, :] <= query_pos[:, None]) & (query_pos[None, :] < length)
        full_mask = jnp.concatenate([jnp.broadcast_to(prefix_mask[None, :], (SUF, PREF)), suffix_mask], axis=1)
        query_heads = queries.reshape(SUF, KV_HEADS, group_size, HEAD).transpose(1, 2, 0, 3)
        key_heads = jnp.concatenate([prefix_key_heads, keys.reshape(SUF, KV_HEADS, HEAD).transpose(1, 0, 2)], axis=1)
        value_heads = jnp.concatenate([prefix_value_heads, values.reshape(SUF, KV_HEADS, HEAD).transpose(1, 0, 2)], axis=1)

        def one_head(head_inputs):
            query_block, key_block, value_block = head_inputs
            scores = jnp.einsum('gpd,rd->gpr', query_block.astype(jnp.float32), key_block.astype(jnp.float32), precision=lax.Precision.HIGHEST) * scale
            scores = jnp.where(full_mask[None], scores, masked_score)
            largest = lax.optimization_barrier(jnp.max(scores, axis=-1, keepdims=True))
            expos = jnp.exp(scores - largest)
            totals = lax.optimization_barrier(jnp.sum(expos, axis=-1, keepdims=True))
            weights = lax.optimization_barrier(expos.astype(jnp.bfloat16)).astype(jnp.float32)
            mixed = jnp.einsum('gpr,rd->gpd', weights, value_block.astype(jnp.float32), precision=lax.Precision.HIGHEST)
            return mixed / totals
        heads_out = lax.map(one_head, (query_heads, key_heads, value_heads))
        return heads_out.transpose(2, 0, 1, 3).reshape(SUF, HEADS * HEAD).astype(jnp.bfloat16)
    outputs = lax.map(one_group, (suffix_q.reshape(N_BRANCH, SUF, HEADS * HEAD), suffix_k.reshape(N_BRANCH, SUF, KV_HEADS * HEAD), suffix_v.reshape(N_BRANCH, SUF, KV_HEADS * HEAD), leaf, suffix_len))
    return outputs.reshape(N_BRANCH * SUF, HEADS * HEAD)
```

```python
import functools
import math

import jax
import jax.numpy as jnp
import numpy as np
from jax import lax
from jax.experimental import pallas as pl
from jax.experimental.pallas import tpu as pltpu
from jax.sharding import PartitionSpec as P

HEAD = 128
GROUP = 8
SLAB = 64
NODES = 12
SLABS = 64
NZ = 16
NX = 4
MESH = pl.DeviceIdType.MESH

rope_base = 500000.0
masked_score = -1e30


def place():
    branch = lax.axis_index("branch")
    tensor = lax.axis_index("tensor")
    return (
        lax.div(branch, 2 * NZ),
        lax.rem(lax.div(branch, 2), NZ),
        lax.rem(branch, 2),
        lax.div(tensor, NX),
        lax.rem(tensor, NX),
    )


def device(y_hi, z, core, y_lo, x):
    return ((y_hi * NZ + z) * 2 + core, y_lo * NX + x)


def slab_base(slab, node_ref, len_ref, parent_ref):
    node = node_ref[slab]

    def climb(unused, carried):
        current, above = carried
        upper = parent_ref[current]
        above = jnp.where(current == 0, above, above | (1 << upper))
        return upper, above

    unused, above = lax.fori_loop(0, NODES - 1, climb, (node, jnp.int32(0)))

    def count(other, total):
        other_node = node_ref[other]
        counts = ((above >> other_node) & 1) > 0
        counts = counts | ((other_node == node) & (other < slab))
        return total + jnp.where(counts, len_ref[other], 0)

    return lax.fori_loop(0, SLABS, count, jnp.int32(0))


def gather_kernel(
    hid,
    key_w,
    value_w,
    node_ref,
    len_ref,
    parent_ref,
    freq_ref,
    kv,
    hbuf,
    wplus,
    wminus,
    sums,
    core_in,
    pair_in,
    turn,
    local_sem,
    a_send,
    a_recv,
    b_send,
    b_recv,
    w_send,
    w_recv,
    s_send,
    s_recv,
    g_send,
    g_recv,
    d_send,
    d_recv,
):
    y_hi, z, core, y_lo, x = place()
    up = device(y_hi, lax.rem(z + 1, NZ), core, y_lo, x)
    down = device(y_hi, lax.rem(z + NZ - 1, NZ), core, y_lo, x)
    sibling = device(y_hi, z, 1 - core, y_lo, x)
    partner = device(1 - y_hi, z, core, y_lo, x)
    homely = y_hi == y_lo

    def remote(src, dst, send, recv, target):
        return pltpu.make_async_remote_copy(
            src_ref=src,
            dst_ref=dst,
            send_sem=send,
            recv_sem=recv,
            device_id=target,
            device_id_type=MESH,
        )

    def beside(step):
        return device(y_hi, z, core, y_lo, lax.rem(x + step, NX))

    barrier = pltpu.get_barrier_semaphore()

    def greet(target):
        pl.semaphore_signal(barrier, inc=1, device_id=target, device_id_type=MESH)

    for target in (up, down, sibling, partner, beside(1), beside(2), beside(3)):
        greet(target)
    for other_y in range(2):
        for other_core in range(2):
            own = homely & (other_y == y_hi) & (other_core == core)

            @pl.when(jnp.logical_not(own))
            def _():
                greet(device(other_y, z, other_core, y_hi, x))

    pl.semaphore_wait(barrier, 11 - homely.astype(jnp.int32))

    def weight_piece(piece):
        source = key_w if piece < 2 else value_w
        return source.at[pl.ds((piece % 2) * 64, 64)]

    def slot(buf, step, piece):
        return buf.at[step, piece // 2, pl.ds((piece % 2) * 64, 64)]

    ways = ((wplus, up, 0), (wminus, down, 1))

    def weight_copy(step, way, piece):
        buf, target, number = ways[way]
        src = weight_piece(piece) if step == 0 else slot(buf, step, piece)
        return remote(
            src,
            slot(buf, step + 1, piece),
            w_send.at[number, step, piece],
            w_recv.at[number, step + 1, piece],
            target,
        )

    reach = (NZ // 2, NZ // 2 - 1)
    for piece in range(4):
        for way in range(2):
            weight_copy(0, way, piece).start()
    own_key = pltpu.make_async_copy(key_w, wplus.at[0, 0], local_sem.at[0])
    own_value = pltpu.make_async_copy(value_w, wplus.at[0, 1], local_sem.at[1])
    own_key.start()
    own_value.start()

    origin = core * 2 + y_hi

    def hidden_copies(other_y, other_core):
        target = device(y_lo, z, other_core, other_y, x)
        own = homely & (other_y == y_lo) & (other_core == core)
        copies = []
        for block in range(4):
            src = hid.at[:, pl.ds((2 * block + other_core) * 128, 128)]
            dst = hbuf.at[x, origin, block]
            far = remote(
                src,
                dst,
                a_send.at[other_y, other_core, block],
                a_recv.at[origin, block],
                target,
            )
            near = pltpu.make_async_copy(src, dst, a_recv.at[origin, block])
            copies.append((far, near))
        return own, copies

    for other_y in range(2):
        for other_core in range(2):
            own, copies = hidden_copies(other_y, other_core)

            @pl.when(own)
            def _():
                for unused, near in copies:
                    near.start()

            @pl.when(jnp.logical_not(own))
            def _():
                for far, unused in copies:
                    far.start()

    def beside_copy(source, step):
        return remote(
            hbuf.at[x, source],
            hbuf.at[x, source],
            b_send.at[step - 1, source],
            b_recv.at[step - 1, source],
            beside(step),
        )

    def pass_on(source):
        for block in range(4):
            there = hbuf.at[x, source, block]
            pltpu.make_async_copy(there, there, a_recv.at[source, block]).wait()
        for step in (1, 3, 2):
            beside_copy(source, step).start()

    def weight_step(step):
        for piece in range(4):
            for way in range(2):
                if step <= reach[way]:
                    weight_copy(step - 1, way, piece).wait_recv()
                    if step < reach[way]:
                        weight_copy(step, way, piece).start()

    first, second = y_lo, 1 - y_lo
    weight_step(1)
    pass_on(first)
    pass_on(2 + first)
    weight_step(2)
    pass_on(second)
    pass_on(2 + second)

    bases = [
        slab_base((half * NZ + z) * 2 + core, node_ref, len_ref, parent_ref) for half in range(2)
    ]
    row = lax.broadcasted_iota(jnp.int32, (2 * SLAB, HEAD), 0)
    lane = lax.broadcasted_iota(jnp.int32, (2 * SLAB, HEAD), 1)
    position = jnp.where(row < SLAB, bases[0] + row, bases[1] + row - SLAB)
    angle = position.astype(jnp.float32) * freq_ref[...]
    turn[0] = jnp.cos(angle)
    sine = jnp.sin(angle)
    turn[1] = jnp.where(lane < HEAD // 2, -sine, sine)

    for step in range(3, NZ // 2 + 1):
        weight_step(step)
    own_key.wait()
    own_value.wait()
    for step in (1, 3, 2):
        for source in range(4):
            there = hbuf.at[lax.rem(x + NX - step, NX), source]
            pltpu.make_async_copy(there, there, b_recv.at[step - 1, source]).wait()

    def product(owner):
        total = None
        for way, buf, start, stop in ((-1, wplus, 0, 9), (1, wminus, 1, 8)):
            for step in range(start, stop):
                origin_z = lax.rem(z + way * step + NZ, NZ)
                column, block = lax.div(origin_z, 4), lax.rem(origin_z, 4)
                rows = jnp.concatenate(
                    [hbuf[column, owner * 2 + half, block] for half in range(2)], axis=0
                )
                both = jnp.concatenate([buf[step, 0], buf[step, 1]], axis=1)
                term = jnp.dot(rows, both, preferred_element_type=jnp.float32)
                total = term if total is None else total + term
        return total

    sums[0] = product(1 - core)
    to_core = remote(sums.at[0], core_in, s_send.at[0], s_recv.at[0], sibling)
    to_core.start()
    mine = product(core)
    to_core.wait_recv()
    sums[1] = mine + core_in[...]
    to_pair = remote(sums.at[1], pair_in, s_send.at[1], s_recv.at[1], partner)
    to_pair.start()
    to_pair.wait_recv()
    total = sums[1] + pair_in[...]
    raw = total[:, :HEAD]
    turned = raw * turn[0] + pltpu.roll(raw, HEAD // 2, 1) * turn[1]
    kv[core, z, 0] = turned.astype(jnp.bfloat16).reshape(2, SLAB, HEAD)
    kv[core, z, 1] = total[:, HEAD:].astype(jnp.bfloat16).reshape(2, SLAB, HEAD)

    def origin_of(way, step):
        return lax.rem(z + (NZ - step if way == 0 else step), NZ)

    def ring_copy(step, way, piece):
        there = kv.at[core, origin_of(way, step), piece // 2, piece % 2]
        return remote(
            there,
            there,
            g_send.at[way, step, piece],
            g_recv.at[way, step + 1, piece],
            (up, down)[way],
        )

    def across_copy(step, way):
        there = kv.at[core, origin_of(way, step)]
        return remote(there, there, d_send.at[way, step], d_recv.at[way, step], sibling)

    def ring_wait(step, way, piece):
        there = kv.at[core, origin_of(way, step), piece // 2, piece % 2]
        pltpu.make_async_copy(there, there, g_recv.at[way, step, piece]).wait()

    for piece in range(4):
        for way in range(2):
            ring_copy(0, way, piece).start()
    across_copy(0, 0).start()
    for step in range(1, NZ // 2 + 1):
        for piece in range(4):
            for way in range(2):
                if step <= reach[way]:
                    ring_wait(step, way, piece)
                    if step < reach[way]:
                        ring_copy(step, way, piece).start()
        for way in range(2):
            if step <= reach[way]:
                across_copy(step, way).start()

    for way in range(2):
        for step in range(0 if way == 0 else 1, reach[way] + 1):
            there = kv.at[1 - core, origin_of(way, step)]
            pltpu.make_async_copy(there, there, d_recv.at[way, step]).wait()
            across_copy(step, way).wait_send()
        for step in range(reach[way]):
            for piece in range(4):
                ring_copy(step, way, piece).wait_send()
                weight_copy(step, way, piece).wait_send()
    for other_y in range(2):
        for other_core in range(2):
            own, copies = hidden_copies(other_y, other_core)

            @pl.when(jnp.logical_not(own))
            def _():
                for far, unused in copies:
                    far.wait_send()

    for step in (1, 3, 2):
        for source in range(4):
            beside_copy(source, step).wait_send()
    to_core.wait_send()
    to_pair.wait_send()


def gather(hid, key_w, value_w, slab_node, slab_len, parent):
    freqs = rope_base ** (-2.0 * np.arange(HEAD // 2, dtype=np.float64) / HEAD)
    freqs = jnp.asarray(np.tile(freqs, 2)[None, :].astype(np.float32))
    dma = pltpu.SemaphoreType.DMA
    hbm = pl.BlockSpec(memory_space=pl.ANY)
    smem = pl.BlockSpec(memory_space=pltpu.SMEM)
    vmem = pl.BlockSpec(memory_space=pltpu.VMEM)
    return pl.pallas_call(
        gather_kernel,
        out_shape=jax.ShapeDtypeStruct((2, NZ, 2, 2, SLAB, HEAD), jnp.bfloat16),
        in_specs=[hbm, hbm, hbm, smem, smem, smem, vmem],
        out_specs=vmem,
        scratch_shapes=[
            pltpu.VMEM((NX, 4, 4, SLAB, 128), jnp.bfloat16),
            pltpu.VMEM((9, 2, 128, 128), jnp.bfloat16),
            pltpu.VMEM((8, 2, 128, 128), jnp.bfloat16),
            pltpu.VMEM((2, 2 * SLAB, 2 * HEAD), jnp.float32),
            pltpu.VMEM((2 * SLAB, 2 * HEAD), jnp.float32),
            pltpu.VMEM((2 * SLAB, 2 * HEAD), jnp.float32),
            pltpu.VMEM((2, 2 * SLAB, HEAD), jnp.float32),
            dma((2,)),
            dma((2, 2, 4)),
            dma((4, 4)),
            dma((3, 4)),
            dma((3, 4)),
            dma((2, 8, 4)),
            dma((2, 9, 4)),
            dma((2,)),
            dma((2,)),
            dma((2, 8, 4)),
            dma((2, 9, 4)),
            dma((2, 9)),
            dma((2, 9)),
        ],
        compiler_params=pltpu.CompilerParams(
            collective_id=0, has_side_effects=True, vmem_limit_bytes=32 << 20
        ),
        name="gather_keys_values",
    )(hid, key_w, value_w, slab_node, slab_len, parent, freqs)


def attend_kernel(
    node_ref,
    len_ref,
    parent_ref,
    leaf_ref,
    suffix_len_ref,
    q_ref,
    sk_ref,
    sv_ref,
    kv_ref,
    out_ref,
    keys,
    values,
    bias,
    scores,
    largest,
    mixed,
    picked,
    live,
):
    def climb(unused, carried):
        current, path = carried
        return parent_ref[current], path | (1 << current)

    unused, path = lax.fori_loop(0, NODES, climb, (leaf_ref[0], jnp.int32(0)))

    def pick(slab, count):
        picked[count] = slab
        live[count] = len_ref[slab]
        return count + ((path >> node_ref[slab]) & 1)

    count = lax.fori_loop(0, SLABS, pick, jnp.int32(0))
    for extra in range(4):
        picked[count + extra] = 0
        live[count + extra] = 0
    chunks = lax.div(count + 3, 4)

    lane = lax.broadcasted_iota(jnp.int32, (8, 4 * SLAB), 1)
    ones = jnp.ones((SLAB, HEAD), jnp.bfloat16)

    def collect(chunk, unused):
        limit = jnp.zeros((8, 4 * SLAB), jnp.int32)
        for part in range(4):
            slab = picked[chunk * 4 + part]
            core, z, y_hi = lax.rem(slab, 2), lax.rem(lax.div(slab, 2), NZ), lax.div(slab, 2 * NZ)
            keys[chunk, pl.ds(part * SLAB, SLAB)] = kv_ref[core, z, 0, y_hi]
            values[chunk, pl.ds(part * SLAB, SLAB), :HEAD] = kv_ref[core, z, 1, y_hi]
            values[chunk, pl.ds(part * SLAB, SLAB), HEAD:] = ones
            limit = jnp.where(lane >= part * SLAB, part * SLAB + live[chunk * 4 + part], limit)
        bias[chunk] = jnp.where(lane < limit, 0.0, masked_score)
        return 0

    lax.fori_loop(0, chunks, collect, 0)

    factor = math.log2(math.e) / math.sqrt(HEAD)
    rows = q_ref.shape[0]
    length = suffix_len_ref[0]
    suffix_keys = sk_ref[...]
    suffix_values = jnp.concatenate([sv_ref[...], jnp.ones_like(sv_ref)], axis=1)
    query_pos = lax.broadcasted_iota(jnp.int32, (rows, rows), 0)
    key_pos = lax.broadcasted_iota(jnp.int32, (rows, rows), 1)
    suffix_mask = (key_pos <= query_pos) & (key_pos < length)

    def against(head, key_block):
        return lax.dot_general(
            q_ref[:, head * HEAD : (head + 1) * HEAD],
            key_block,
            (((1,), (1,)), ((), ())),
            preferred_element_type=jnp.float32,
        )

    def fold(score):
        return jnp.maximum(score[:, :HEAD], score[:, HEAD:])

    def weigh(score, top, value_block):
        weights = jnp.exp2(score * factor - top).astype(jnp.bfloat16)
        return jnp.dot(weights, value_block, preferred_element_type=jnp.float32)

    for head in range(GROUP + 1):
        now, before = head % 2, (head + 1) % 2
        if head > 0:
            top = jnp.max(largest[before], axis=1, keepdims=True) * factor
            mixed[...] = weigh(scores[before, SLABS // 4], top, suffix_values)
        if head < GROUP:
            score = jnp.where(suffix_mask, against(head, suffix_keys), masked_score)
            scores[now, SLABS // 4] = score
            largest[now] = fold(score)

        def visit(chunk, unused):
            if head < GROUP:
                score = against(head, keys[chunk]) + bias[chunk][:1]
                scores[now, chunk] = score
                largest[now] = jnp.maximum(largest[now], fold(score))
            if head > 0:
                mixed[...] += weigh(scores[before, chunk], top, values[chunk])
            return 0

        lax.fori_loop(0, chunks, visit, 0)
        if head > 0:
            result = mixed[:, :HEAD] / mixed[:, HEAD:]
            out_ref[:, (head - 1) * HEAD : head * HEAD] = result.astype(jnp.bfloat16)


def attend(slab_node, slab_len, parent, leaf, suffix_len, q, sk, sv, kv):
    smem = pl.BlockSpec(memory_space=pltpu.SMEM)
    vmem = pl.BlockSpec(memory_space=pltpu.VMEM)
    rows = q.shape[0]
    blocks = SLABS // 4
    return pl.pallas_call(
        attend_kernel,
        out_shape=jax.ShapeDtypeStruct(q.shape, jnp.bfloat16),
        in_specs=[smem] * 5 + [vmem] * 4,
        out_specs=vmem,
        scratch_shapes=[
            pltpu.VMEM((blocks, 4 * SLAB, HEAD), jnp.bfloat16),
            pltpu.VMEM((blocks, 4 * SLAB, 2 * HEAD), jnp.bfloat16),
            pltpu.VMEM((blocks, 8, 4 * SLAB), jnp.float32),
            pltpu.VMEM((2, blocks + 1, rows, 4 * SLAB), jnp.float32),
            pltpu.VMEM((2, rows, HEAD), jnp.float32),
            pltpu.VMEM((rows, 2 * HEAD), jnp.float32),
            pltpu.SMEM((SLABS + 4,), jnp.int32),
            pltpu.SMEM((SLABS + 4,), jnp.int32),
        ],
        compiler_params=pltpu.CompilerParams(vmem_limit_bytes=48 << 20),
        name="attend",
    )(slab_node, slab_len, parent, leaf, suffix_len, q, sk, sv, kv)


def local(
    prefix_hidden,
    key_weight,
    value_weight,
    suffix_q,
    suffix_k,
    suffix_v,
    slab_node,
    slab_len,
    parent,
    leaf,
    suffix_len,
):
    kv = gather(prefix_hidden, key_weight, value_weight, slab_node, slab_len, parent)
    return attend(
        slab_node, slab_len, parent, leaf, suffix_len, suffix_q, suffix_k, suffix_v, kv
    )


def solution(mesh):
    return jax.shard_map(
        local,
        mesh=mesh,
        in_specs=(
            P("branch", "tensor"),
            P("branch", "tensor"),
            P("branch", "tensor"),
            P("branch", "tensor"),
            P("branch", "tensor"),
            P("branch", "tensor"),
            P(),
            P(),
            P(),
            P("branch"),
            P("branch"),
        ),
        out_specs=P("branch", "tensor"),
        check_vma=False,
    )
```

```python
import functools
import math

import jax
import jax.numpy as jnp
import numpy as np
from jax import lax
from jax.experimental import pallas as pl
from jax.experimental.pallas import tpu as pltpu
from jax.sharding import PartitionSpec as P

HEAD = 128
GROUP = 8
SLAB = 64
NODES = 12
SLABS = 64
NZ = 16
NX = 4
PART = 8
MESH = pl.DeviceIdType.MESH

rope_base = 500000.0
masked_score = -1e30


def place():
    branch = lax.axis_index("branch")
    tensor = lax.axis_index("tensor")
    return (
        lax.div(branch, 2 * NZ),
        lax.rem(lax.div(branch, 2), NZ),
        lax.rem(branch, 2),
        lax.div(tensor, NX),
        lax.rem(tensor, NX),
    )


def device(y_hi, z, core, y_lo, x):
    return ((y_hi * NZ + z) * 2 + core, y_lo * NX + x)


def slab_base(slab, node_ref, len_ref, parent_ref):
    node = node_ref[slab]

    def climb(unused, carried):
        current, above = carried
        upper = parent_ref[current]
        above = jnp.where(current == 0, above, above | (1 << upper))
        return upper, above

    unused, above = lax.fori_loop(0, NODES - 1, climb, (node, jnp.int32(0)))

    def count(other, total):
        other_node = node_ref[other]
        counts = ((above >> other_node) & 1) > 0
        counts = counts | ((other_node == node) & (other < slab))
        return total + jnp.where(counts, len_ref[other], 0)

    return lax.fori_loop(0, SLABS, count, jnp.int32(0))


TREE = {1: 0, 2: 0, 3: 1, 4: 2, 5: 3, 6: 4, 7: 5, 8: 6}
REACH = (NZ // 2, NZ // 2 - 1)


def children(distance, way):
    return [far for far, near in TREE.items() if near == distance and far <= REACH[way]]


def gather_kernel(
    hid,
    key_w,
    value_w,
    node_hbm,
    len_hbm,
    parent_hbm,
    freq_hbm,
    kv,
    hbuf,
    wbuf,
    sums,
    core_in,
    pair_in,
    turn,
    freq,
    node_ref,
    len_ref,
    parent_ref,
    local_sem,
    a_send,
    a_recv,
    b_send,
    b_recv,
    w_send,
    w_recv,
    s_send,
    s_recv,
    g_send,
    g_recv,
    d_send,
    d_recv,
):
    y_hi, z, core, y_lo, x = place()
    sibling = device(y_hi, z, 1 - core, y_lo, x)
    partner = device(1 - y_hi, z, core, y_lo, x)
    homely = y_hi == y_lo

    def along(step):
        return device(y_hi, lax.rem(z + step + NZ, NZ), core, y_lo, x)

    def beside(step):
        return device(y_hi, z, core, y_lo, lax.rem(x + step + NX, NX))

    def remote(src, dst, send, recv, target):
        return pltpu.make_async_remote_copy(
            src_ref=src,
            dst_ref=dst,
            send_sem=send,
            recv_sem=recv,
            device_id=target,
            device_id_type=MESH,
        )

    barrier = pltpu.get_barrier_semaphore()

    def greet(target):
        pl.semaphore_signal(barrier, inc=1, device_id=target, device_id_type=MESH)

    strides = sorted({far - near for far, near in TREE.items()})
    near_by = [sibling, partner, beside(1), beside(-1)]
    for stride in strides:
        near_by += [along(stride), along(-stride)]
    for target in near_by:
        greet(target)
    for other_y in range(2):
        for other_core in range(2):
            own = homely & (other_y == y_hi) & (other_core == core)

            @pl.when(jnp.logical_not(own))
            def _():
                greet(device(other_y, z, other_core, y_hi, x))

    small = [
        pltpu.make_async_copy(src, dst, local_sem.at[number])
        for number, (src, dst) in enumerate(
            (
                (node_hbm, node_ref),
                (len_hbm, len_ref),
                (parent_hbm, parent_ref),
                (freq_hbm, freq),
                (key_w, wbuf.at[0, 0, 0]),
                (value_w, wbuf.at[0, 0, 1]),
            )
        )
    ]
    for copy in small:
        copy.start()
    for copy in small:
        copy.wait()

    bases = [
        slab_base((half * NZ + z) * 2 + core, node_ref, len_ref, parent_ref) for half in range(2)
    ]
    row = lax.broadcasted_iota(jnp.int32, (2 * SLAB, HEAD), 0)
    lane = lax.broadcasted_iota(jnp.int32, (2 * SLAB, HEAD), 1)
    position = jnp.where(row < SLAB, bases[0] + row, bases[1] + row - SLAB)
    angle = position.astype(jnp.float32) * freq[...]
    turn[0] = jnp.cos(angle)
    sine = jnp.sin(angle)
    turn[1] = jnp.where(lane < HEAD // 2, -sine, sine)

    pl.semaphore_wait(barrier, 4 + len(near_by) - homely.astype(jnp.int32))

    def weight_copy(distance, way, piece):
        near = TREE[distance]
        src = wbuf.at[way if near else 0, near, piece]
        return remote(
            src,
            wbuf.at[way, distance, piece],
            w_send.at[way, distance, piece],
            w_recv.at[way, distance, piece],
            along((distance - near) * (1 - 2 * way)),
        )

    def weight_go(distance):
        for piece in range(2):
            for way in range(2):
                if distance > REACH[way]:
                    continue
                if distance:
                    weight_copy(distance, way, piece).wait_recv()
                for far in children(distance, way):
                    weight_copy(far, way, piece).start()

    weight_go(0)

    origin = core * 2 + y_hi

    def hidden_copies(other_y, other_core):
        target = device(y_lo, z, other_core, other_y, x)
        own = homely & (other_y == y_lo) & (other_core == core)
        copies = []
        for block in range(4):
            src = hid.at[:, pl.ds((2 * block + other_core) * 128, 128)]
            dst = hbuf.at[x, origin, block]
            there = a_recv.at[origin, block]
            far = remote(src, dst, a_send.at[other_y, other_core, block], there, target)
            copies.append((far, src, dst, there))
        return own, copies

    for other_y in range(2):
        for other_core in range(2):
            own, copies = hidden_copies(other_y, other_core)

            @pl.when(own)
            def _():
                for unused, src, dst, there in copies:
                    pltpu.make_async_copy(src, dst, there).start()

            @pl.when(jnp.logical_not(own))
            def _():
                for far, *unused in copies:
                    far.start()

    def beside_copy(column, source, way, hop):
        there = hbuf.at[lax.rem(column + NX, NX), source]
        return remote(
            there,
            there,
            b_send.at[hop, way, source],
            b_recv.at[hop, way, source],
            beside(1 - 2 * way),
        )

    def pass_on(source):
        for block in range(4):
            there = hbuf.at[x, source, block]
            pltpu.make_async_copy(there, there, a_recv.at[source, block]).wait()
        for way in range(2):
            beside_copy(x, source, way, 0).start()

    def beside_wait(source, way, hop):
        column = x + (hop + 1) * (2 * way - 1)
        there = hbuf.at[lax.rem(column + NX, NX), source]
        pltpu.make_async_copy(there, there, b_recv.at[hop, way, source]).wait()

    def pass_opposite(half):
        for way in range(2):
            source = way * 2 + half
            beside_wait(source, way, 0)
            beside_copy(x + 2 * way - 1, source, way, 1).start()

    def product(owner, piece):
        total = None
        for way in range(2):
            for distance in range(way, REACH[way] + 1):
                origin_z = lax.rem(z + (2 * way - 1) * distance + NZ, NZ)
                column, block = lax.div(origin_z, 4), lax.rem(origin_z, 4)
                rows = jnp.concatenate(
                    [hbuf[column, owner * 2 + half, block] for half in range(2)], axis=0
                )
                term = jnp.dot(
                    rows, wbuf[way, distance, piece], preferred_element_type=jnp.float32
                )
                total = term if total is None else total + term
        return total

    def to_core(piece):
        return remote(
            sums.at[piece, 0], core_in.at[piece], s_send.at[piece, 0], s_recv.at[piece, 0], sibling
        )

    def to_pair(piece):
        return remote(
            sums.at[piece, 1], pair_in.at[piece], s_send.at[piece, 1], s_recv.at[piece, 1], partner
        )

    def multiply(piece):
        sums[piece, 0] = product(1 - core, piece)
        to_core(piece).start()
        sums[piece, 1] = product(core, piece)

    def add_core(piece):
        to_core(piece).wait_recv()
        sums[piece, 1] = sums[piece, 1] + core_in[piece]
        to_pair(piece).start()

    def add_pair(piece):
        to_pair(piece).wait_recv()
        total = sums[piece, 1] + pair_in[piece]
        if piece == 0:
            total = total * turn[0] + pltpu.roll(total, HEAD // 2, 1) * turn[1]
        kv[core, z, piece] = total.astype(jnp.bfloat16).reshape(2, SLAB, HEAD)
        ring_go(0, piece)

    def source_z(distance, way):
        return lax.rem(z + (2 * way - 1) * distance + NZ, NZ)

    def ring_copy(distance, way, piece):
        near = TREE[distance]
        there = kv.at[core, source_z(near, way), piece]
        return remote(
            there,
            there,
            g_send.at[way, distance, piece],
            g_recv.at[way, distance, piece],
            along((distance - near) * (1 - 2 * way)),
        )

    def across_copy(distance, way, piece):
        there = kv.at[core, source_z(distance, way), piece]
        return remote(
            there,
            there,
            d_send.at[way, distance, piece],
            d_recv.at[way, distance, piece],
            sibling,
        )

    def ring_go(distance, piece):
        for way in range(2):
            if distance > REACH[way]:
                continue
            if distance:
                there = kv.at[core, source_z(distance, way), piece]
                pltpu.make_async_copy(there, there, g_recv.at[way, distance, piece]).wait()
            for far in children(distance, way):
                ring_copy(far, way, piece).start()

    def across_go(distance, piece):
        for way in range(2):
            if way <= distance <= REACH[way]:
                across_copy(distance, way, piece).start()

    first, second = y_lo, 1 - y_lo
    weight_go(1)
    pass_on(first)
    pass_on(2 + first)
    weight_go(2)
    pass_on(second)
    pass_on(2 + second)
    weight_go(3)
    weight_go(4)
    pass_opposite(first)
    weight_go(5)
    pass_opposite(second)
    weight_go(6)
    for half in (first, second):
        for way in range(2):
            beside_wait((1 - way) * 2 + half, way, 0)
    weight_go(7)
    weight_go(8)
    for half in (first, second):
        for way in range(2):
            beside_wait(way * 2 + half, way, 1)
    multiply(0)
    multiply(1)
    add_core(0)
    add_core(1)
    add_pair(0)
    add_pair(1)
    for distance in range(9):
        for piece in range(2):
            if distance:
                ring_go(distance, piece)
        for piece in range(2):
            across_go(distance, piece)

    for way in range(2):
        for distance in range(way, REACH[way] + 1):
            for piece in range(2):
                there = kv.at[1 - core, source_z(distance, way), piece]
                pltpu.make_async_copy(there, there, d_recv.at[way, distance, piece]).wait()
                across_copy(distance, way, piece).wait_send()
                if distance:
                    ring_copy(distance, way, piece).wait_send()
                    weight_copy(distance, way, piece).wait_send()
        for source in range(4):
            beside_copy(x, source, way, 0).wait_send()
        for half in range(2):
            beside_copy(x, way * 2 + half, way, 1).wait_send()
    for other_y in range(2):
        for other_core in range(2):
            own, copies = hidden_copies(other_y, other_core)

            @pl.when(jnp.logical_not(own))
            def _():
                for far, *unused in copies:
                    far.wait_send()

    for piece in range(2):
        to_core(piece).wait_send()
        to_pair(piece).wait_send()


def gather(hid, key_w, value_w, slab_node, slab_len, parent):
    freqs = rope_base ** (-2.0 * np.arange(HEAD // 2, dtype=np.float64) / HEAD)
    freqs = jnp.asarray(np.tile(freqs, 2)[None, :].astype(np.float32))
    dma = pltpu.SemaphoreType.DMA
    hbm = pl.BlockSpec(memory_space=pltpu.HBM)
    vmem = pl.BlockSpec(memory_space=pltpu.VMEM)
    return pl.pallas_call(
        gather_kernel,
        out_shape=jax.ShapeDtypeStruct((2, NZ, 2, 2, SLAB, HEAD), jnp.bfloat16),
        in_specs=[hbm] * 7,
        out_specs=vmem,
        scratch_shapes=[
            pltpu.VMEM((NX, 4, 4, SLAB, 128), jnp.bfloat16),
            pltpu.VMEM((2, 9, 2, 128, 128), jnp.bfloat16),
            pltpu.VMEM((2, 2, 2 * SLAB, HEAD), jnp.float32),
            pltpu.VMEM((2, 2 * SLAB, HEAD), jnp.float32),
            pltpu.VMEM((2, 2 * SLAB, HEAD), jnp.float32),
            pltpu.VMEM((2, 2 * SLAB, HEAD), jnp.float32),
            pltpu.VMEM((1, HEAD), jnp.float32),
            pltpu.SMEM((SLABS,), jnp.int32),
            pltpu.SMEM((SLABS,), jnp.int32),
            pltpu.SMEM((NODES,), jnp.int32),
            dma((6,)),
            dma((2, 2, 4)),
            dma((4, 4)),
            dma((2, 2, 4)),
            dma((2, 2, 4)),
            dma((2, 9, 2)),
            dma((2, 9, 2)),
            dma((2, 2)),
            dma((2, 2)),
            dma((2, 9, 2)),
            dma((2, 9, 2)),
            dma((2, 9, 2)),
            dma((2, 9, 2)),
        ],
        compiler_params=pltpu.CompilerParams(
            collective_id=0, has_side_effects=True, vmem_limit_bytes=32 << 20
        ),
        name="gather_keys_values",
    )(
        *[
            pltpu.with_memory_space_constraint(array, pltpu.HBM)
            for array in (hid, key_w, value_w, slab_node, slab_len, parent, freqs)
        ]
    )


def attend_kernel(
    node_ref,
    len_ref,
    parent_ref,
    leaf_ref,
    suffix_len_ref,
    q_ref,
    sk_ref,
    sv_ref,
    kv_ref,
    out_ref,
    keys,
    values,
    bias,
    suffix_scores,
    scores,
    largest,
    mixed,
    picked,
    live,
):
    def climb(unused, carried):
        current, path = carried
        return parent_ref[current], path | (1 << current)

    unused, path = lax.fori_loop(0, NODES, climb, (leaf_ref[0], jnp.int32(0)))

    def pick(slab, count):
        picked[count] = slab
        live[count] = len_ref[slab]
        return count + ((path >> node_ref[slab]) & 1)

    count = lax.fori_loop(0, SLABS, pick, jnp.int32(0))
    for extra in range(PART):
        picked[count + extra] = 0
        live[count + extra] = 0
    chunks = lax.div(count + PART - 1, PART)

    lane = lax.broadcasted_iota(jnp.int32, (8, PART * SLAB), 1)
    ones = jnp.ones((SLAB, HEAD), jnp.bfloat16)

    def collect(chunk, unused):
        limit = jnp.zeros((8, PART * SLAB), jnp.int32)
        for part in range(PART):
            slab = picked[chunk * PART + part]
            core, z, y_hi = lax.rem(slab, 2), lax.rem(lax.div(slab, 2), NZ), lax.div(slab, 2 * NZ)
            keys[chunk, pl.ds(part * SLAB, SLAB)] = kv_ref[core, z, 0, y_hi]
            values[chunk, pl.ds(part * SLAB, SLAB), :HEAD] = kv_ref[core, z, 1, y_hi]
            values[chunk, pl.ds(part * SLAB, SLAB), HEAD:] = ones
            limit = jnp.where(lane >= part * SLAB, part * SLAB + live[chunk * PART + part], limit)
        bias[chunk] = jnp.where(lane < limit, 0.0, masked_score)
        return 0

    lax.fori_loop(0, chunks, collect, 0)

    factor = math.log2(math.e) / math.sqrt(HEAD)
    rows = q_ref.shape[0]
    length = suffix_len_ref[0]
    suffix_values = jnp.concatenate([sv_ref[...], jnp.ones_like(sv_ref)], axis=1)
    query_pos = lax.broadcasted_iota(jnp.int32, (rows, rows), 0)
    key_pos = lax.broadcasted_iota(jnp.int32, (rows, rows), 1)
    suffix_mask = (key_pos <= query_pos) & (key_pos < length)

    def against(head, key_block):
        return lax.dot_general(
            q_ref[:, head * HEAD : (head + 1) * HEAD],
            key_block,
            (((1,), (1,)), ((), ())),
            preferred_element_type=jnp.float32,
        )

    def fold(score):
        most = score[:, :HEAD]
        for start in range(HEAD, score.shape[1], HEAD):
            most = jnp.maximum(most, score[:, start : start + HEAD])
        return most

    def weigh(score, top, value_block):
        wide = jnp.concatenate([top] * (score.shape[1] // HEAD), axis=1)
        weights = jnp.exp2(score * factor - wide).astype(jnp.bfloat16)
        return jnp.dot(weights, value_block, preferred_element_type=jnp.float32)

    for head in range(GROUP):
        score = jnp.where(suffix_mask, against(head, sk_ref[...]), masked_score)
        suffix_scores[head] = score
        largest[head] = fold(score)

    def score_chunk(chunk, unused):
        for head in range(GROUP):
            score = against(head, keys[chunk]) + bias[chunk][:1]
            scores[chunk, head] = score
            largest[head] = jnp.maximum(largest[head], fold(score))
        return 0

    lax.fori_loop(0, chunks, score_chunk, 0)

    for head in range(GROUP):
        top = jnp.max(largest[head], axis=1, keepdims=True) * factor
        largest[head] = jnp.broadcast_to(top, (rows, HEAD))
        mixed[head] = weigh(suffix_scores[head], largest[head], suffix_values)

    def weigh_chunk(chunk, unused):
        for head in range(GROUP):
            mixed[head] += weigh(scores[chunk, head], largest[head], values[chunk])
        return 0

    lax.fori_loop(0, chunks, weigh_chunk, 0)
    for head in range(GROUP):
        result = mixed[head, :, :HEAD] / mixed[head, :, HEAD:]
        out_ref[:, head * HEAD : (head + 1) * HEAD] = result.astype(jnp.bfloat16)


def attend(slab_node, slab_len, parent, leaf, suffix_len, q, sk, sv, kv):
    smem = pl.BlockSpec(memory_space=pltpu.SMEM)
    vmem = pl.BlockSpec(memory_space=pltpu.VMEM)
    rows = q.shape[0]
    blocks = SLABS // PART
    wide = PART * SLAB
    return pl.pallas_call(
        attend_kernel,
        out_shape=jax.ShapeDtypeStruct(q.shape, jnp.bfloat16),
        in_specs=[smem] * 5 + [vmem] * 4,
        out_specs=vmem,
        scratch_shapes=[
            pltpu.VMEM((blocks, wide, HEAD), jnp.bfloat16),
            pltpu.VMEM((blocks, wide, 2 * HEAD), jnp.bfloat16),
            pltpu.VMEM((blocks, 8, wide), jnp.float32),
            pltpu.VMEM((GROUP, rows, rows), jnp.float32),
            pltpu.VMEM((blocks, GROUP, rows, wide), jnp.float32),
            pltpu.VMEM((GROUP, rows, HEAD), jnp.float32),
            pltpu.VMEM((GROUP, rows, 2 * HEAD), jnp.float32),
            pltpu.SMEM((SLABS + PART,), jnp.int32),
            pltpu.SMEM((SLABS + PART,), jnp.int32),
        ],
        compiler_params=pltpu.CompilerParams(vmem_limit_bytes=54 << 20),
        name="attend",
    )(slab_node, slab_len, parent, leaf, suffix_len, q, sk, sv, kv)


def local(
    prefix_hidden,
    key_weight,
    value_weight,
    suffix_q,
    suffix_k,
    suffix_v,
    slab_node,
    slab_len,
    parent,
    leaf,
    suffix_len,
):
    kv = gather(prefix_hidden, key_weight, value_weight, slab_node, slab_len, parent)
    return attend(
        slab_node, slab_len, parent, leaf, suffix_len, suffix_q, suffix_k, suffix_v, kv
    )


def solution(mesh):
    return jax.shard_map(
        local,
        mesh=mesh,
        in_specs=(
            P("branch", "tensor"),
            P("branch", "tensor"),
            P("branch", "tensor"),
            P("branch", "tensor"),
            P("branch", "tensor"),
            P("branch", "tensor"),
            P(),
            P(),
            P(),
            P("branch"),
            P("branch"),
        ),
        out_specs=P("branch", "tensor"),
        check_vma=False,
    )
```

```python
import functools
import math

import jax
import jax.numpy as jnp
import numpy as np
from jax import lax
from jax.experimental import pallas as pl
from jax.experimental.pallas import tpu as pltpu
from jax.sharding import PartitionSpec as P

HEAD = 128
GROUP = 8
SLAB = 64
NODES = 12
SLABS = 64
NZ = 16
NX = 4
TOGETHER = 4
MESH = pl.DeviceIdType.MESH

rope_base = 500000.0
masked_score = -1e30


def place():
    branch = lax.axis_index("branch")
    tensor = lax.axis_index("tensor")
    return (
        lax.div(branch, 2 * NZ),
        lax.rem(lax.div(branch, 2), NZ),
        lax.rem(branch, 2),
        lax.div(tensor, NX),
        lax.rem(tensor, NX),
    )


def device(y_hi, z, core, y_lo, x):
    return ((y_hi * NZ + z) * 2 + core, y_lo * NX + x)


def slab_base(slab, node_ref, len_ref, parent_ref):
    node = node_ref[slab]

    def climb(unused, carried):
        current, above = carried
        upper = parent_ref[current]
        above = jnp.where(current == 0, above, above | (1 << upper))
        return upper, above

    unused, above = lax.fori_loop(0, NODES - 1, climb, (node, jnp.int32(0)))

    def count(other, total):
        other_node = node_ref[other]
        counts = ((above >> other_node) & 1) > 0
        counts = counts | ((other_node == node) & (other < slab))
        return total + jnp.where(counts, len_ref[other], 0)

    return lax.fori_loop(0, SLABS, count, jnp.int32(0))


TREE = {2: 0, 1: 0, 4: 2, 3: 2, 6: 4, 5: 4, 8: 6, 7: 6}
REACH = (NZ // 2, NZ // 2 - 1)


def children(distance, way):
    return [far for far, near in TREE.items() if near == distance and far <= REACH[way]]


def tree_kernel(
    hid,
    key_w,
    value_w,
    node_hbm,
    len_hbm,
    parent_hbm,
    leaf_ref,
    suffix_len_ref,
    freq_hbm,
    q_hbm,
    sk_hbm,
    sv_hbm,
    out_ref,
    kv,
    q_ref,
    sk_ref,
    sv_ref,
    scores,
    largest,
    top,
    mixed,
    hbuf,
    wbuf,
    sums,
    core_in,
    pair_in,
    turn,
    freq,
    node_ref,
    len_ref,
    parent_ref,
    local_sem,
    q_sem,
    a_send,
    a_recv,
    b_send,
    b_recv,
    w_send,
    w_recv,
    s_send,
    s_recv,
    g_send,
    g_recv,
    d_send,
    d_recv,
):
    y_hi, z, core, y_lo, x = place()
    sibling = device(y_hi, z, 1 - core, y_lo, x)
    partner = device(1 - y_hi, z, core, y_lo, x)
    homely = y_hi == y_lo

    def along(step):
        return device(y_hi, lax.rem(z + step + NZ, NZ), core, y_lo, x)

    def beside(step):
        return device(y_hi, z, core, y_lo, lax.rem(x + step + NX, NX))

    def remote(src, dst, send, recv, target):
        return pltpu.make_async_remote_copy(
            src_ref=src,
            dst_ref=dst,
            send_sem=send,
            recv_sem=recv,
            device_id=target,
            device_id_type=MESH,
        )

    barrier = pltpu.get_barrier_semaphore()

    def greet(target):
        pl.semaphore_signal(barrier, inc=1, device_id=target, device_id_type=MESH)

    strides = sorted({far - near for far, near in TREE.items()})
    near_by = [sibling, partner, beside(1), beside(-1)]
    for stride in strides:
        near_by += [along(stride), along(-stride)]
    for target in near_by:
        greet(target)
    for other_y in range(2):
        for other_core in range(2):
            own = homely & (other_y == y_hi) & (other_core == core)

            @pl.when(jnp.logical_not(own))
            def _():
                greet(device(other_y, z, other_core, y_hi, x))

    small = [
        pltpu.make_async_copy(src, dst, local_sem.at[number])
        for number, (src, dst) in enumerate(
            (
                (node_hbm, node_ref),
                (len_hbm, len_ref),
                (parent_hbm, parent_ref),
                (freq_hbm, freq),
                (key_w, wbuf.at[0, 0, 0]),
                (value_w, wbuf.at[0, 0, 1]),
            )
        )
    ]
    large = [
        pltpu.make_async_copy(q_hbm.at[:, pl.ds(head * HEAD, HEAD)], q_ref.at[head], q_sem.at[head])
        for head in range(GROUP)
    ]
    large.append(pltpu.make_async_copy(sk_hbm, sk_ref, q_sem.at[GROUP]))
    large.append(pltpu.make_async_copy(sv_hbm, sv_ref, q_sem.at[GROUP + 1]))
    for copy in small + large:
        copy.start()
    for copy in small:
        copy.wait()

    bases = [
        slab_base((half * NZ + z) * 2 + core, node_ref, len_ref, parent_ref) for half in range(2)
    ]
    row = lax.broadcasted_iota(jnp.int32, (2 * SLAB, HEAD), 0)
    lane = lax.broadcasted_iota(jnp.int32, (2 * SLAB, HEAD), 1)
    position = jnp.where(row < SLAB, bases[0] + row, bases[1] + row - SLAB)
    angle = position.astype(jnp.float32) * freq[...]
    turn[0] = jnp.cos(angle)
    sine = jnp.sin(angle)
    turn[1] = jnp.where(lane < HEAD // 2, -sine, sine)

    pl.semaphore_wait(barrier, 4 + len(near_by) - homely.astype(jnp.int32))

    def weight_copy(distance, way, piece):
        near = TREE[distance]
        src = wbuf.at[way if near else 0, near, piece]
        return remote(
            src,
            wbuf.at[way, distance, piece],
            w_send.at[way, distance, piece],
            w_recv.at[way, distance, piece],
            along((distance - near) * (1 - 2 * way)),
        )

    def weight_go(distance):
        for piece in range(2):
            for way in range(2):
                if distance > REACH[way]:
                    continue
                if distance:
                    weight_copy(distance, way, piece).wait_recv()
                for far in children(distance, way):
                    weight_copy(far, way, piece).start()

    weight_go(0)

    origin = core * 2 + y_hi

    def hidden_copies(other_y, other_core):
        target = device(y_lo, z, other_core, other_y, x)
        own = homely & (other_y == y_lo) & (other_core == core)
        copies = []
        for block in range(4):
            src = hid.at[:, pl.ds((2 * block + other_core) * 128, 128)]
            dst = hbuf.at[x, origin, block]
            there = a_recv.at[origin, block]
            far = remote(src, dst, a_send.at[other_y, other_core, block], there, target)
            copies.append((far, src, dst, there))
        return own, copies

    for other_y in range(2):
        for other_core in range(2):
            own, copies = hidden_copies(other_y, other_core)

            @pl.when(own)
            def _():
                for unused, src, dst, there in copies:
                    pltpu.make_async_copy(src, dst, there).start()

            @pl.when(jnp.logical_not(own))
            def _():
                for far, *unused in copies:
                    far.start()

    def beside_copy(column, source, way, hop):
        there = hbuf.at[lax.rem(column + NX, NX), source]
        return remote(
            there,
            there,
            b_send.at[hop, way, source],
            b_recv.at[hop, way, source],
            beside(1 - 2 * way),
        )

    def pass_on(source):
        for block in range(4):
            there = hbuf.at[x, source, block]
            pltpu.make_async_copy(there, there, a_recv.at[source, block]).wait()
        for way in range(2):
            beside_copy(x, source, way, 0).start()

    def beside_wait(source, way, hop):
        column = x + (hop + 1) * (2 * way - 1)
        there = hbuf.at[lax.rem(column + NX, NX), source]
        pltpu.make_async_copy(there, there, b_recv.at[hop, way, source]).wait()

    def pass_opposite(half):
        for way in range(2):
            source = way * 2 + half
            beside_wait(source, way, 0)
            beside_copy(x + 2 * way - 1, source, way, 1).start()

    def product(owner, piece):
        total = None
        for way in range(2):
            for distance in range(way, REACH[way] + 1):
                origin_z = lax.rem(z + (2 * way - 1) * distance + NZ, NZ)
                column, block = lax.div(origin_z, 4), lax.rem(origin_z, 4)
                rows = jnp.concatenate(
                    [hbuf[column, owner * 2 + half, block] for half in range(2)], axis=0
                )
                term = jnp.dot(
                    rows, wbuf[way, distance, piece], preferred_element_type=jnp.float32
                )
                total = term if total is None else total + term
        return total

    def to_core(piece):
        return remote(
            sums.at[piece, 0], core_in.at[piece], s_send.at[piece, 0], s_recv.at[piece, 0], sibling
        )

    def to_pair(piece):
        return remote(
            sums.at[piece, 1], pair_in.at[piece], s_send.at[piece, 1], s_recv.at[piece, 1], partner
        )

    def multiply(piece):
        sums[piece, 0] = product(1 - core, piece)
        to_core(piece).start()
        sums[piece, 1] = product(core, piece)

    def add_core(piece):
        to_core(piece).wait_recv()
        sums[piece, 1] = sums[piece, 1] + core_in[piece]
        to_pair(piece).start()

    def add_pair(piece):
        to_pair(piece).wait_recv()
        total = sums[piece, 1] + pair_in[piece]
        if piece == 0:
            total = total * turn[0] + pltpu.roll(total, HEAD // 2, 1) * turn[1]
        kv[core, z, piece] = total.astype(jnp.bfloat16).reshape(2, SLAB, HEAD)
        ring_go(0, piece)

    def source_z(distance, way):
        return lax.rem(z + (2 * way - 1) * distance + NZ, NZ)

    def ring_copy(distance, way, piece):
        near = TREE[distance]
        there = kv.at[core, source_z(near, way), piece]
        return remote(
            there,
            there,
            g_send.at[way, distance, piece],
            g_recv.at[way, distance, piece],
            along((distance - near) * (1 - 2 * way)),
        )

    def across_copy(distance, way, piece):
        there = kv.at[core, source_z(distance, way), piece]
        return remote(
            there,
            there,
            d_send.at[way, distance, piece],
            d_recv.at[way, distance, piece],
            sibling,
        )

    def ring_go(distance, piece):
        for way in range(2):
            if distance > REACH[way]:
                continue
            if distance:
                there = kv.at[core, source_z(distance, way), piece]
                pltpu.make_async_copy(there, there, g_recv.at[way, distance, piece]).wait()
            for far in children(distance, way):
                ring_copy(far, way, piece).start()

    def across_go(distance, piece):
        for way in range(2):
            if way <= distance <= REACH[way]:
                across_copy(distance, way, piece).start()

    factor = math.log2(math.e) / math.sqrt(HEAD)
    rows = q_ref.shape[1]

    def climb(unused, carried):
        current, path = carried
        return parent_ref[current], path | (1 << current)

    unused, path = lax.fori_loop(0, NODES, climb, (leaf_ref[0], jnp.int32(0)))

    def heads(body):
        def some(step, unused):
            for number in range(TOGETHER):
                body(step * TOGETHER + number)
            return 0

        lax.fori_loop(0, GROUP // TOGETHER, some, 0)

    def against(head, key_block):
        return lax.dot_general(
            q_ref[head], key_block, (((1,), (1,)), ((), ())), preferred_element_type=jnp.float32
        )

    def fold(score):
        most = score[:, :HEAD]
        for start in range(HEAD, score.shape[1], HEAD):
            most = jnp.maximum(most, score[:, start : start + HEAD])
        return most

    def weigh(score, most, value_block):
        wide = jnp.concatenate([most] * (score.shape[1] // HEAD), axis=1)
        weights = jnp.exp2(score * factor - wide).astype(jnp.bfloat16)
        wider = jnp.concatenate([value_block, jnp.ones_like(value_block)], axis=1)
        return jnp.dot(weights, wider, preferred_element_type=jnp.float32)

    def block_of(owner, places, piece):
        return jnp.concatenate(
            [kv[owner, source_z(d, way), piece].reshape(2 * SLAB, HEAD) for way, d in places], axis=0
        )

    def score_block(number, owner, places):
        width = len(places) * 2 * SLAB
        position = lax.broadcasted_iota(jnp.int32, (1, width), 1)
        limit = jnp.zeros((1, width), jnp.int32)
        for place_number, (way, d) in enumerate(places):
            for half in range(2):
                slab = (half * NZ + source_z(d, way)) * 2 + owner
                live = ((path >> node_ref[slab]) & 1) * len_ref[slab]
                start = (2 * place_number + half) * SLAB
                limit = jnp.where(position >= start, start + live, limit)
        bias = jnp.where(position < limit, 0.0, masked_score)
        key_block = block_of(owner, places, 0)

        def body(head):
            score = against(head, key_block) + bias
            scores[number, head, :, :width] = score
            most = fold(score)
            largest[head] = jnp.maximum(largest[head], most) if number else most

        heads(body)

    def raise_top():
        def body(head):
            most = jnp.max(largest[head], axis=1, keepdims=True) * factor
            before = top[head]
            after = jnp.maximum(before, most)
            top[head] = after
            shrink = jnp.exp2(before - after)
            mixed[head] = mixed[head] * jnp.concatenate([shrink, shrink], axis=1)

        heads(body)

    def weigh_block(number, owner, places):
        width = len(places) * 2 * SLAB
        value_block = block_of(owner, places, 1)

        def body(head):
            mixed[head] += weigh(scores[number, head, :, :width], top[head], value_block)

        heads(body)

    def attend_suffix():
        for copy in large:
            copy.wait()
        query_pos = lax.broadcasted_iota(jnp.int32, (rows, rows), 0)
        key_pos = lax.broadcasted_iota(jnp.int32, (rows, rows), 1)
        mask = (key_pos <= query_pos) & (key_pos < suffix_len_ref[0])
        key_block, value_block = sk_ref[...], sv_ref[...]

        def body(head):
            score = jnp.where(mask, against(head, key_block), masked_score)
            most = jnp.max(score, axis=1, keepdims=True) * factor
            top[head] = jnp.broadcast_to(most, (rows, HEAD))
            mixed[head] = weigh(score, top[head], value_block)

        heads(body)

    def across_wait(places):
        for way, d in places:
            for piece in range(2):
                there = kv.at[1 - core, source_z(d, way), piece]
                pltpu.make_async_copy(there, there, d_recv.at[way, d, piece]).wait()

    def attend_places(places):
        score_block(0, core, places)
        across_wait(places)
        score_block(1, 1 - core, places)
        raise_top()
        weigh_block(0, core, places)
        weigh_block(1, 1 - core, places)

    first, second = y_lo, 1 - y_lo
    weight_go(2)
    pass_on(first)
    pass_on(2 + first)
    weight_go(1)
    weight_go(4)
    pass_on(second)
    pass_on(2 + second)
    weight_go(3)
    pass_opposite(first)
    attend_suffix()
    weight_go(6)
    weight_go(5)
    pass_opposite(second)
    for half in (first, second):
        for way in range(2):
            beside_wait((1 - way) * 2 + half, way, 0)
    weight_go(8)
    weight_go(7)
    for half in (first, second):
        for way in range(2):
            beside_wait(way * 2 + half, way, 1)
    multiply(0)
    multiply(1)
    add_core(0)
    add_core(1)
    add_pair(0)
    add_pair(1)
    across_go(0, 0)
    across_go(0, 1)
    attend_places(((0, 0),))
    for stage in range(1, 5):
        for distance in (2 * stage, 2 * stage - 1):
            for piece in range(2):
                ring_go(distance, piece)
            for piece in range(2):
                across_go(distance, piece)
        attend_places(
            [
                (way, distance)
                for way in range(2)
                for distance in (2 * stage - 1, 2 * stage)
                if distance <= REACH[way]
            ]
        )
    for head in range(GROUP):
        result = mixed[head, :, :HEAD] / mixed[head, :, HEAD:]
        out_ref[:, head * HEAD : (head + 1) * HEAD] = result.astype(jnp.bfloat16)

    for way in range(2):
        for distance in range(way, REACH[way] + 1):
            for piece in range(2):
                across_copy(distance, way, piece).wait_send()
                if distance:
                    ring_copy(distance, way, piece).wait_send()
                    weight_copy(distance, way, piece).wait_send()
        for source in range(4):
            beside_copy(x, source, way, 0).wait_send()
        for half in range(2):
            beside_copy(x, way * 2 + half, way, 1).wait_send()
    for other_y in range(2):
        for other_core in range(2):
            own, copies = hidden_copies(other_y, other_core)

            @pl.when(jnp.logical_not(own))
            def _():
                for far, *unused in copies:
                    far.wait_send()

    for piece in range(2):
        to_core(piece).wait_send()
        to_pair(piece).wait_send()


def attend(hid, key_w, value_w, q, sk, sv, slab_node, slab_len, parent, leaf, suffix_len):
    freqs = rope_base ** (-2.0 * np.arange(HEAD // 2, dtype=np.float64) / HEAD)
    freqs = jnp.asarray(np.tile(freqs, 2)[None, :].astype(np.float32))
    dma = pltpu.SemaphoreType.DMA
    hbm = pl.BlockSpec(memory_space=pltpu.HBM)
    vmem = pl.BlockSpec(memory_space=pltpu.VMEM)
    rows = q.shape[0]
    smem = pl.BlockSpec(memory_space=pltpu.SMEM)

    def stay(*arrays):
        return [pltpu.with_memory_space_constraint(array, pltpu.HBM) for array in arrays]

    operands = [
        *stay(hid, key_w, value_w, slab_node, slab_len, parent),
        leaf,
        suffix_len,
        *stay(freqs, q, sk, sv),
    ]
    return pl.pallas_call(
        tree_kernel,
        out_shape=jax.ShapeDtypeStruct(q.shape, jnp.bfloat16),
        in_specs=[hbm] * 6 + [smem] * 2 + [hbm] * 4,
        out_specs=vmem,
        scratch_shapes=[
            pltpu.VMEM((2, NZ, 2, 2, SLAB, HEAD), jnp.bfloat16),
            pltpu.VMEM((GROUP, rows, HEAD), jnp.bfloat16),
            pltpu.VMEM((rows, HEAD), jnp.bfloat16),
            pltpu.VMEM((rows, HEAD), jnp.bfloat16),
            pltpu.VMEM((2, GROUP, rows, 8 * SLAB), jnp.float32),
            pltpu.VMEM((GROUP, rows, HEAD), jnp.float32),
            pltpu.VMEM((GROUP, rows, HEAD), jnp.float32),
            pltpu.VMEM((GROUP, rows, 2 * HEAD), jnp.float32),
            pltpu.VMEM((NX, 4, 4, SLAB, 128), jnp.bfloat16),
            pltpu.VMEM((2, 9, 2, 128, 128), jnp.bfloat16),
            pltpu.VMEM((2, 2, 2 * SLAB, HEAD), jnp.float32),
            pltpu.VMEM((2, 2 * SLAB, HEAD), jnp.float32),
            pltpu.VMEM((2, 2 * SLAB, HEAD), jnp.float32),
            pltpu.VMEM((2, 2 * SLAB, HEAD), jnp.float32),
            pltpu.VMEM((1, HEAD), jnp.float32),
            pltpu.SMEM((SLABS,), jnp.int32),
            pltpu.SMEM((SLABS,), jnp.int32),
            pltpu.SMEM((NODES,), jnp.int32),
            dma((6,)),
            dma((GROUP + 2,)),
            dma((2, 2, 4)),
            dma((4, 4)),
            dma((2, 2, 4)),
            dma((2, 2, 4)),
            dma((2, 9, 2)),
            dma((2, 9, 2)),
            dma((2, 2)),
            dma((2, 2)),
            dma((2, 9, 2)),
            dma((2, 9, 2)),
            dma((2, 9, 2)),
            dma((2, 9, 2)),
        ],
        compiler_params=pltpu.CompilerParams(
            collective_id=0, has_side_effects=True, vmem_limit_bytes=48 << 20
        ),
        cost_estimate=pl.CostEstimate(
            flops=5_000_000_000, bytes_accessed=4_000_000, transcendentals=9_000_000
        ),
        name="attend_tree",
    )(*operands)


def local(
    prefix_hidden,
    key_weight,
    value_weight,
    suffix_q,
    suffix_k,
    suffix_v,
    slab_node,
    slab_len,
    parent,
    leaf,
    suffix_len,
):
    return attend(
        prefix_hidden,
        key_weight,
        value_weight,
        suffix_q,
        suffix_k,
        suffix_v,
        slab_node,
        slab_len,
        parent,
        leaf,
        suffix_len,
    )


def solution(mesh):
    return jax.shard_map(
        local,
        mesh=mesh,
        in_specs=(
            P("branch", "tensor"),
            P("branch", "tensor"),
            P("branch", "tensor"),
            P("branch", "tensor"),
            P("branch", "tensor"),
            P("branch", "tensor"),
            P(),
            P(),
            P(),
            P("branch"),
            P("branch"),
        ),
        out_specs=P("branch", "tensor"),
        check_vma=False,
    )
```

```python
import functools
import math

import jax
import jax.numpy as jnp
import numpy as np
from jax import lax
from jax.experimental import pallas as pl
from jax.experimental.pallas import tpu as pltpu
from jax.sharding import PartitionSpec as P

HEAD = 128
GROUP = 8
SLAB = 64
NODES = 12
SLABS = 64
NZ = 16
NX = 4
TOGETHER = 8
MESH = pl.DeviceIdType.MESH

rope_base = 500000.0
masked_score = -1e30


def place():
    branch = lax.axis_index("branch")
    tensor = lax.axis_index("tensor")
    return (
        lax.div(branch, 2 * NZ),
        lax.rem(lax.div(branch, 2), NZ),
        lax.rem(branch, 2),
        lax.div(tensor, NX),
        lax.rem(tensor, NX),
    )


def device(y_hi, z, core, y_lo, x):
    return ((y_hi * NZ + z) * 2 + core, y_lo * NX + x)


def slab_base(slab, node_ref, len_ref, parent_ref):
    node = node_ref[slab]

    def climb(unused, carried):
        current, above = carried
        upper = parent_ref[current]
        above = jnp.where(current == 0, above, above | (1 << upper))
        return upper, above

    unused, above = lax.fori_loop(0, NODES - 1, climb, (node, jnp.int32(0)))

    def count(other, total):
        other_node = node_ref[other]
        counts = ((above >> other_node) & 1) > 0
        counts = counts | ((other_node == node) & (other < slab))
        return total + jnp.where(counts, len_ref[other], 0)

    return lax.fori_loop(0, SLABS, count, jnp.int32(0))


TREE = {2: 0, 1: 0, 4: 2, 3: 2, 6: 4, 5: 4, 8: 6, 7: 6}
REACH = (NZ // 2, NZ // 2 - 1)


def children(distance, way):
    return [far for far, near in TREE.items() if near == distance and far <= REACH[way]]


def tree_kernel(
    hid,
    key_w,
    value_w,
    node_hbm,
    len_hbm,
    parent_hbm,
    leaf_ref,
    suffix_len_ref,
    freq_hbm,
    q_hbm,
    sk_hbm,
    sv_hbm,
    out_ref,
    kv,
    q_ref,
    sk_ref,
    sv_ref,
    scores,
    largest,
    top,
    mixed,
    hbuf,
    wbuf,
    sums,
    core_in,
    pair_in,
    turn,
    freq,
    node_ref,
    len_ref,
    parent_ref,
    local_sem,
    q_sem,
    a_send,
    a_recv,
    b_send,
    b_recv,
    w_send,
    w_recv,
    s_send,
    s_recv,
    g_send,
    g_recv,
    d_send,
    d_recv,
):
    y_hi, z, core, y_lo, x = place()
    sibling = device(y_hi, z, 1 - core, y_lo, x)
    partner = device(1 - y_hi, z, core, y_lo, x)
    homely = y_hi == y_lo

    def along(step):
        return device(y_hi, lax.rem(z + step + NZ, NZ), core, y_lo, x)

    def beside(step):
        return device(y_hi, z, core, y_lo, lax.rem(x + step + NX, NX))

    def remote(src, dst, send, recv, target):
        return pltpu.make_async_remote_copy(
            src_ref=src,
            dst_ref=dst,
            send_sem=send,
            recv_sem=recv,
            device_id=target,
            device_id_type=MESH,
        )

    barrier = pltpu.get_barrier_semaphore()

    def greet(target):
        pl.semaphore_signal(barrier, inc=1, device_id=target, device_id_type=MESH)

    strides = sorted({far - near for far, near in TREE.items()})
    near_by = [sibling, partner, beside(1), beside(-1)]
    for stride in strides:
        near_by += [along(stride), along(-stride)]
    for target in near_by:
        greet(target)
    for other_y in range(2):
        for other_core in range(2):
            own = homely & (other_y == y_hi) & (other_core == core)

            @pl.when(jnp.logical_not(own))
            def _():
                greet(device(other_y, z, other_core, y_hi, x))

    small = [
        pltpu.make_async_copy(src, dst, local_sem.at[number])
        for number, (src, dst) in enumerate(
            (
                (node_hbm, node_ref),
                (len_hbm, len_ref),
                (parent_hbm, parent_ref),
                (freq_hbm, freq),
                (key_w, wbuf.at[0, 0, 0]),
                (value_w, wbuf.at[0, 0, 1]),
            )
        )
    ]
    large = [
        pltpu.make_async_copy(q_hbm.at[:, pl.ds(head * HEAD, HEAD)], q_ref.at[head], q_sem.at[head])
        for head in range(GROUP)
    ]
    large.append(pltpu.make_async_copy(sk_hbm, sk_ref, q_sem.at[GROUP]))
    large.append(pltpu.make_async_copy(sv_hbm, sv_ref, q_sem.at[GROUP + 1]))
    for copy in small + large:
        copy.start()
    for copy in small:
        copy.wait()

    bases = [
        slab_base((half * NZ + z) * 2 + core, node_ref, len_ref, parent_ref) for half in range(2)
    ]
    row = lax.broadcasted_iota(jnp.int32, (2 * SLAB, HEAD), 0)
    lane = lax.broadcasted_iota(jnp.int32, (2 * SLAB, HEAD), 1)
    position = jnp.where(row < SLAB, bases[0] + row, bases[1] + row - SLAB)
    angle = position.astype(jnp.float32) * freq[...]
    turn[0] = jnp.cos(angle)
    sine = jnp.sin(angle)
    turn[1] = jnp.where(lane < HEAD // 2, -sine, sine)

    pl.semaphore_wait(barrier, 4 + len(near_by) - homely.astype(jnp.int32))

    def weight_copy(distance, way, piece):
        near = TREE[distance]
        src = wbuf.at[way if near else 0, near, piece]
        return remote(
            src,
            wbuf.at[way, distance, piece],
            w_send.at[way, distance, piece],
            w_recv.at[way, distance, piece],
            along((distance - near) * (1 - 2 * way)),
        )

    def weight_go(distance):
        for piece in range(2):
            for way in range(2):
                if distance > REACH[way]:
                    continue
                if distance:
                    weight_copy(distance, way, piece).wait_recv()
                for far in children(distance, way):
                    weight_copy(far, way, piece).start()

    weight_go(0)

    origin = core * 2 + y_hi

    def hidden_copies(other_y, other_core):
        target = device(y_lo, z, other_core, other_y, x)
        own = homely & (other_y == y_lo) & (other_core == core)
        copies = []
        for block in range(4):
            src = hid.at[:, pl.ds((2 * block + other_core) * 128, 128)]
            dst = hbuf.at[x, origin, block]
            there = a_recv.at[origin, block]
            far = remote(src, dst, a_send.at[other_y, other_core, block], there, target)
            copies.append((far, src, dst, there))
        return own, copies

    for other_y in range(2):
        for other_core in range(2):
            own, copies = hidden_copies(other_y, other_core)

            @pl.when(own)
            def _():
                for unused, src, dst, there in copies:
                    pltpu.make_async_copy(src, dst, there).start()

            @pl.when(jnp.logical_not(own))
            def _():
                for far, *unused in copies:
                    far.start()

    def beside_copy(column, source, way, hop):
        there = hbuf.at[lax.rem(column + NX, NX), source]
        return remote(
            there,
            there,
            b_send.at[hop, way, source],
            b_recv.at[hop, way, source],
            beside(1 - 2 * way),
        )

    def pass_on(source):
        for block in range(4):
            there = hbuf.at[x, source, block]
            pltpu.make_async_copy(there, there, a_recv.at[source, block]).wait()
        for way in range(2):
            beside_copy(x, source, way, 0).start()

    def beside_wait(source, way, hop):
        column = x + (hop + 1) * (2 * way - 1)
        there = hbuf.at[lax.rem(column + NX, NX), source]
        pltpu.make_async_copy(there, there, b_recv.at[hop, way, source]).wait()

    def pass_opposite(half):
        for way in range(2):
            source = way * 2 + half
            beside_wait(source, way, 0)
            beside_copy(x + 2 * way - 1, source, way, 1).start()

    def product(owner, piece):
        total = None
        for way in range(2):
            for distance in range(way, REACH[way] + 1):
                origin_z = lax.rem(z + (2 * way - 1) * distance + NZ, NZ)
                column, block = lax.div(origin_z, 4), lax.rem(origin_z, 4)
                rows = jnp.concatenate(
                    [hbuf[column, owner * 2 + half, block] for half in range(2)], axis=0
                )
                term = jnp.dot(
                    rows, wbuf[way, distance, piece], preferred_element_type=jnp.float32
                )
                total = term if total is None else total + term
        return total

    def to_core(piece):
        return remote(
            sums.at[piece, 0], core_in.at[piece], s_send.at[piece, 0], s_recv.at[piece, 0], sibling
        )

    def to_pair(piece):
        return remote(
            sums.at[piece, 1], pair_in.at[piece], s_send.at[piece, 1], s_recv.at[piece, 1], partner
        )

    def multiply(piece):
        sums[piece, 0] = product(1 - core, piece)
        to_core(piece).start()
        sums[piece, 1] = product(core, piece)

    def add_core(piece):
        to_core(piece).wait_recv()
        sums[piece, 1] = sums[piece, 1] + core_in[piece]
        to_pair(piece).start()

    def add_pair(piece):
        to_pair(piece).wait_recv()
        total = sums[piece, 1] + pair_in[piece]
        if piece == 0:
            total = total * turn[0] + pltpu.roll(total, HEAD // 2, 1) * turn[1]
        kv[core, z, piece] = total.astype(jnp.bfloat16).reshape(2, SLAB, HEAD)
        ring_go(0, piece)

    def source_z(distance, way):
        return lax.rem(z + (2 * way - 1) * distance + NZ, NZ)

    def ring_copy(distance, way, piece):
        near = TREE[distance]
        there = kv.at[core, source_z(near, way), piece]
        return remote(
            there,
            there,
            g_send.at[way, distance, piece],
            g_recv.at[way, distance, piece],
            along((distance - near) * (1 - 2 * way)),
        )

    def across_copy(distance, way, piece):
        there = kv.at[core, source_z(distance, way), piece]
        return remote(
            there,
            there,
            d_send.at[way, distance, piece],
            d_recv.at[way, distance, piece],
            sibling,
        )

    def ring_go(distance, piece):
        for way in range(2):
            if distance > REACH[way]:
                continue
            if distance:
                there = kv.at[core, source_z(distance, way), piece]
                pltpu.make_async_copy(there, there, g_recv.at[way, distance, piece]).wait()
            for far in children(distance, way):
                ring_copy(far, way, piece).start()

    def across_go(distance, piece):
        for way in range(2):
            if way <= distance <= REACH[way]:
                across_copy(distance, way, piece).start()

    factor = math.log2(math.e) / math.sqrt(HEAD)
    rows = q_ref.shape[1]

    def climb(unused, carried):
        current, path = carried
        return parent_ref[current], path | (1 << current)

    unused, path = lax.fori_loop(0, NODES, climb, (leaf_ref[0], jnp.int32(0)))

    def heads(body):
        def some(step, unused):
            for number in range(TOGETHER):
                body(step * TOGETHER + number)
            return 0

        lax.fori_loop(0, GROUP // TOGETHER, some, 0)

    def against(head, key_block):
        return lax.dot_general(
            q_ref[head], key_block, (((1,), (1,)), ((), ())), preferred_element_type=jnp.float32
        )

    def fold(score):
        most = score[:, :HEAD]
        for start in range(HEAD, score.shape[1], HEAD):
            most = jnp.maximum(most, score[:, start : start + HEAD])
        return most

    def weigh(score, most, value_block):
        wide = jnp.concatenate([most] * (score.shape[1] // HEAD), axis=1)
        weights = jnp.exp2(score * factor - wide).astype(jnp.bfloat16)
        wider = jnp.concatenate([value_block, jnp.ones_like(value_block)], axis=1)
        return jnp.dot(weights, wider, preferred_element_type=jnp.float32)

    def block_of(owner, places, piece):
        return jnp.concatenate(
            [kv[owner, source_z(d, way), piece].reshape(2 * SLAB, HEAD) for way, d in places], axis=0
        )

    def score_block(number, owner, places):
        width = len(places) * 2 * SLAB
        position = lax.broadcasted_iota(jnp.int32, (1, width), 1)
        limit = jnp.zeros((1, width), jnp.int32)
        for place_number, (way, d) in enumerate(places):
            for half in range(2):
                slab = (half * NZ + source_z(d, way)) * 2 + owner
                live = ((path >> node_ref[slab]) & 1) * len_ref[slab]
                start = (2 * place_number + half) * SLAB
                limit = jnp.where(position >= start, start + live, limit)
        bias = jnp.where(position < limit, 0.0, masked_score)
        key_block = block_of(owner, places, 0)

        def body(head):
            score = against(head, key_block) + bias
            scores[number, head, :, :width] = score
            most = fold(score)
            largest[head] = jnp.maximum(largest[head], most) if number else most

        heads(body)

    def raise_top():
        def body(head):
            most = jnp.max(largest[head], axis=1, keepdims=True) * factor
            before = top[head]
            after = jnp.maximum(before, most)
            top[head] = after
            shrink = jnp.exp2(before - after)
            mixed[head] = mixed[head] * jnp.concatenate([shrink, shrink], axis=1)

        heads(body)

    def weigh_block(number, owner, places):
        width = len(places) * 2 * SLAB
        value_block = block_of(owner, places, 1)

        def body(head):
            mixed[head] += weigh(scores[number, head, :, :width], top[head], value_block)

        heads(body)

    def attend_suffix():
        for copy in large:
            copy.wait()
        query_pos = lax.broadcasted_iota(jnp.int32, (rows, rows), 0)
        key_pos = lax.broadcasted_iota(jnp.int32, (rows, rows), 1)
        mask = (key_pos <= query_pos) & (key_pos < suffix_len_ref[0])
        key_block, value_block = sk_ref[...], sv_ref[...]

        def body(head):
            score = jnp.where(mask, against(head, key_block), masked_score)
            most = jnp.max(score, axis=1, keepdims=True) * factor
            top[head] = jnp.broadcast_to(most, (rows, HEAD))
            mixed[head] = weigh(score, top[head], value_block)

        heads(body)

    def across_wait(places):
        for way, d in places:
            for piece in range(2):
                there = kv.at[1 - core, source_z(d, way), piece]
                pltpu.make_async_copy(there, there, d_recv.at[way, d, piece]).wait()

    def attend_places(places):
        score_block(0, core, places)
        across_wait(places)
        score_block(1, 1 - core, places)
        raise_top()
        weigh_block(0, core, places)
        weigh_block(1, 1 - core, places)

    first, second = y_lo, 1 - y_lo
    weight_go(2)
    pass_on(first)
    pass_on(2 + first)
    weight_go(1)
    weight_go(4)
    pass_on(second)
    pass_on(2 + second)
    weight_go(3)
    pass_opposite(first)
    attend_suffix()
    weight_go(6)
    weight_go(5)
    pass_opposite(second)
    for half in (first, second):
        for way in range(2):
            beside_wait((1 - way) * 2 + half, way, 0)
    weight_go(8)
    weight_go(7)
    for half in (first, second):
        for way in range(2):
            beside_wait(way * 2 + half, way, 1)
    multiply(0)
    multiply(1)
    add_core(0)
    add_core(1)
    add_pair(0)
    add_pair(1)
    across_go(0, 0)
    across_go(0, 1)
    attend_places(((0, 0),))
    for stage in range(1, 5):
        for distance in (2 * stage, 2 * stage - 1):
            for piece in range(2):
                ring_go(distance, piece)
            for piece in range(2):
                across_go(distance, piece)
        attend_places(
            [
                (way, distance)
                for way in range(2)
                for distance in (2 * stage - 1, 2 * stage)
                if distance <= REACH[way]
            ]
        )
    for head in range(GROUP):
        result = mixed[head, :, :HEAD] / mixed[head, :, HEAD:]
        out_ref[:, head * HEAD : (head + 1) * HEAD] = result.astype(jnp.bfloat16)

    for way in range(2):
        for distance in range(way, REACH[way] + 1):
            for piece in range(2):
                across_copy(distance, way, piece).wait_send()
                if distance:
                    ring_copy(distance, way, piece).wait_send()
                    weight_copy(distance, way, piece).wait_send()
        for source in range(4):
            beside_copy(x, source, way, 0).wait_send()
        for half in range(2):
            beside_copy(x, way * 2 + half, way, 1).wait_send()
    for other_y in range(2):
        for other_core in range(2):
            own, copies = hidden_copies(other_y, other_core)

            @pl.when(jnp.logical_not(own))
            def _():
                for far, *unused in copies:
                    far.wait_send()

    for piece in range(2):
        to_core(piece).wait_send()
        to_pair(piece).wait_send()


def attend(hid, key_w, value_w, q, sk, sv, slab_node, slab_len, parent, leaf, suffix_len):
    freqs = rope_base ** (-2.0 * np.arange(HEAD // 2, dtype=np.float64) / HEAD)
    freqs = jnp.asarray(np.tile(freqs, 2)[None, :].astype(np.float32))
    dma = pltpu.SemaphoreType.DMA
    hbm = pl.BlockSpec(memory_space=pltpu.HBM)
    vmem = pl.BlockSpec(memory_space=pltpu.VMEM)
    rows = q.shape[0]
    smem = pl.BlockSpec(memory_space=pltpu.SMEM)

    def stay(*arrays):
        return [pltpu.with_memory_space_constraint(array, pltpu.HBM) for array in arrays]

    operands = [
        *stay(hid, key_w, value_w, slab_node, slab_len, parent),
        leaf,
        suffix_len,
        *stay(freqs, q, sk, sv),
    ]
    return pl.pallas_call(
        tree_kernel,
        out_shape=jax.ShapeDtypeStruct(q.shape, jnp.bfloat16),
        in_specs=[hbm] * 6 + [smem] * 2 + [hbm] * 4,
        out_specs=vmem,
        scratch_shapes=[
            pltpu.VMEM((2, NZ, 2, 2, SLAB, HEAD), jnp.bfloat16),
            pltpu.VMEM((GROUP, rows, HEAD), jnp.bfloat16),
            pltpu.VMEM((rows, HEAD), jnp.bfloat16),
            pltpu.VMEM((rows, HEAD), jnp.bfloat16),
            pltpu.VMEM((2, GROUP, rows, 8 * SLAB), jnp.float32),
            pltpu.VMEM((GROUP, rows, HEAD), jnp.float32),
            pltpu.VMEM((GROUP, rows, HEAD), jnp.float32),
            pltpu.VMEM((GROUP, rows, 2 * HEAD), jnp.float32),
            pltpu.VMEM((NX, 4, 4, SLAB, 128), jnp.bfloat16),
            pltpu.VMEM((2, 9, 2, 128, 128), jnp.bfloat16),
            pltpu.VMEM((2, 2, 2 * SLAB, HEAD), jnp.float32),
            pltpu.VMEM((2, 2 * SLAB, HEAD), jnp.float32),
            pltpu.VMEM((2, 2 * SLAB, HEAD), jnp.float32),
            pltpu.VMEM((2, 2 * SLAB, HEAD), jnp.float32),
            pltpu.VMEM((1, HEAD), jnp.float32),
            pltpu.SMEM((SLABS,), jnp.int32),
            pltpu.SMEM((SLABS,), jnp.int32),
            pltpu.SMEM((NODES,), jnp.int32),
            dma((6,)),
            dma((GROUP + 2,)),
            dma((2, 2, 4)),
            dma((4, 4)),
            dma((2, 2, 4)),
            dma((2, 2, 4)),
            dma((2, 9, 2)),
            dma((2, 9, 2)),
            dma((2, 2)),
            dma((2, 2)),
            dma((2, 9, 2)),
            dma((2, 9, 2)),
            dma((2, 9, 2)),
            dma((2, 9, 2)),
        ],
        compiler_params=pltpu.CompilerParams(
            collective_id=0, has_side_effects=True, vmem_limit_bytes=48 << 20
        ),
        cost_estimate=pl.CostEstimate(
            flops=5_000_000_000, bytes_accessed=4_000_000, transcendentals=9_000_000
        ),
        name="attend_tree",
    )(*operands)


def local(
    prefix_hidden,
    key_weight,
    value_weight,
    suffix_q,
    suffix_k,
    suffix_v,
    slab_node,
    slab_len,
    parent,
    leaf,
    suffix_len,
):
    return attend(
        prefix_hidden,
        key_weight,
        value_weight,
        suffix_q,
        suffix_k,
        suffix_v,
        slab_node,
        slab_len,
        parent,
        leaf,
        suffix_len,
    )


def solution(mesh):
    return jax.shard_map(
        local,
        mesh=mesh,
        in_specs=(
            P("branch", "tensor"),
            P("branch", "tensor"),
            P("branch", "tensor"),
            P("branch", "tensor"),
            P("branch", "tensor"),
            P("branch", "tensor"),
            P(),
            P(),
            P(),
            P("branch"),
            P("branch"),
        ),
        out_specs=P("branch", "tensor"),
        check_vma=False,
    )
```

```python
import functools
import math

import jax
import jax.numpy as jnp
import numpy as np
from jax import lax
from jax.experimental import pallas as pl
from jax.experimental.pallas import tpu as pltpu
from jax.sharding import PartitionSpec as P

HEAD = 128
GROUP = 8
SLAB = 64
NODES = 12
SLABS = 64
NZ = 16
NX = 4
TOGETHER = 8
MESH = pl.DeviceIdType.MESH

rope_base = 500000.0
masked_score = -1e30


def place():
    branch = lax.axis_index("branch")
    tensor = lax.axis_index("tensor")
    return (
        lax.div(branch, 2 * NZ),
        lax.rem(lax.div(branch, 2), NZ),
        lax.rem(branch, 2),
        lax.div(tensor, NX),
        lax.rem(tensor, NX),
    )


def device(y_hi, z, core, y_lo, x):
    return ((y_hi * NZ + z) * 2 + core, y_lo * NX + x)


def slab_base(slab, node_ref, len_ref, parent_ref):
    node = node_ref[slab]

    def climb(unused, carried):
        current, above = carried
        upper = parent_ref[current]
        above = jnp.where(current == 0, above, above | (1 << upper))
        return upper, above

    unused, above = lax.fori_loop(0, NODES - 1, climb, (node, jnp.int32(0)))

    def count(other, total):
        other_node = node_ref[other]
        counts = ((above >> other_node) & 1) > 0
        counts = counts | ((other_node == node) & (other < slab))
        return total + jnp.where(counts, len_ref[other], 0)

    return lax.fori_loop(0, SLABS, count, jnp.int32(0))


TREE = {2: 0, 1: 0, 4: 2, 3: 2, 6: 4, 5: 4, 8: 6, 7: 6}
REACH = (NZ // 2, NZ // 2 - 1)


def children(distance, way):
    return [far for far, near in TREE.items() if near == distance and far <= REACH[way]]


def tree_kernel(
    hid,
    key_w,
    value_w,
    node_hbm,
    len_hbm,
    parent_hbm,
    leaf_ref,
    suffix_len_ref,
    freq_hbm,
    q_hbm,
    sk_hbm,
    sv_hbm,
    out_ref,
    kv,
    q_ref,
    sk_ref,
    sv_ref,
    scores,
    largest,
    top,
    mixed,
    hbuf,
    wbuf,
    sums,
    core_in,
    pair_in,
    turn,
    freq,
    node_ref,
    len_ref,
    parent_ref,
    local_sem,
    q_sem,
    a_send,
    a_recv,
    b_send,
    b_recv,
    w_send,
    w_recv,
    s_send,
    s_recv,
    g_send,
    g_recv,
    d_send,
    d_recv,
):
    y_hi, z, core, y_lo, x = place()
    sibling = device(y_hi, z, 1 - core, y_lo, x)
    partner = device(1 - y_hi, z, core, y_lo, x)
    homely = y_hi == y_lo

    def along(step):
        return device(y_hi, lax.rem(z + step + NZ, NZ), core, y_lo, x)

    def beside(step):
        return device(y_hi, z, core, y_lo, lax.rem(x + step + NX, NX))

    def remote(src, dst, send, recv, target):
        return pltpu.make_async_remote_copy(
            src_ref=src,
            dst_ref=dst,
            send_sem=send,
            recv_sem=recv,
            device_id=target,
            device_id_type=MESH,
        )

    barrier = pltpu.get_barrier_semaphore()

    def greet(target):
        pl.semaphore_signal(barrier, inc=1, device_id=target, device_id_type=MESH)

    strides = sorted({far - near for far, near in TREE.items()})
    near_by = [sibling, partner, beside(1), beside(-1)]
    for stride in strides:
        near_by += [along(stride), along(-stride)]
    for target in near_by:
        greet(target)
    for other_y in range(2):
        for other_core in range(2):
            own = homely & (other_y == y_hi) & (other_core == core)

            @pl.when(jnp.logical_not(own))
            def _():
                greet(device(other_y, z, other_core, y_hi, x))

    small = [
        pltpu.make_async_copy(src, dst, local_sem.at[number])
        for number, (src, dst) in enumerate(
            (
                (node_hbm, node_ref),
                (len_hbm, len_ref),
                (parent_hbm, parent_ref),
                (freq_hbm, freq),
                (key_w, wbuf.at[0, 0, 0]),
                (value_w, wbuf.at[0, 0, 1]),
            )
        )
    ]
    large = [
        pltpu.make_async_copy(q_hbm.at[:, pl.ds(head * HEAD, HEAD)], q_ref.at[head], q_sem.at[head])
        for head in range(GROUP)
    ]
    large.append(pltpu.make_async_copy(sk_hbm, sk_ref, q_sem.at[GROUP]))
    large.append(pltpu.make_async_copy(sv_hbm, sv_ref, q_sem.at[GROUP + 1]))
    for copy in small + large:
        copy.start()
    for copy in small:
        copy.wait()

    bases = [
        slab_base((half * NZ + z) * 2 + core, node_ref, len_ref, parent_ref) for half in range(2)
    ]
    row = lax.broadcasted_iota(jnp.int32, (2 * SLAB, HEAD), 0)
    lane = lax.broadcasted_iota(jnp.int32, (2 * SLAB, HEAD), 1)
    position = jnp.where(row < SLAB, bases[0] + row, bases[1] + row - SLAB)
    angle = position.astype(jnp.float32) * freq[...]
    turn[0] = jnp.cos(angle)
    sine = jnp.sin(angle)
    turn[1] = jnp.where(lane < HEAD // 2, -sine, sine)

    pl.semaphore_wait(barrier, 4 + len(near_by) - homely.astype(jnp.int32))

    def weight_copy(distance, way, piece):
        near = TREE[distance]
        src = wbuf.at[way if near else 0, near, piece]
        return remote(
            src,
            wbuf.at[way, distance, piece],
            w_send.at[way, distance, piece],
            w_recv.at[way, distance, piece],
            along((distance - near) * (1 - 2 * way)),
        )

    def weight_go(distance):
        for piece in range(2):
            for way in range(2):
                if distance > REACH[way]:
                    continue
                if distance:
                    weight_copy(distance, way, piece).wait_recv()
                for far in children(distance, way):
                    weight_copy(far, way, piece).start()

    weight_go(0)

    origin = core * 2 + y_hi

    def hidden_copies(other_y, other_core):
        target = device(y_lo, z, other_core, other_y, x)
        own = homely & (other_y == y_lo) & (other_core == core)
        copies = []
        for block in range(4):
            src = hid.at[:, pl.ds((2 * block + other_core) * 128, 128)]
            dst = hbuf.at[x, origin, block]
            there = a_recv.at[origin, block]
            far = remote(src, dst, a_send.at[other_y, other_core, block], there, target)
            copies.append((far, src, dst, there))
        return own, copies

    for other_y in range(2):
        for other_core in range(2):
            own, copies = hidden_copies(other_y, other_core)

            @pl.when(own)
            def _():
                for unused, src, dst, there in copies:
                    pltpu.make_async_copy(src, dst, there).start()

            @pl.when(jnp.logical_not(own))
            def _():
                for far, *unused in copies:
                    far.start()

    def beside_copy(column, source, way, hop):
        there = hbuf.at[lax.rem(column + NX, NX), source]
        return remote(
            there,
            there,
            b_send.at[hop, way, source],
            b_recv.at[hop, way, source],
            beside(1 - 2 * way),
        )

    def pass_on(source):
        for block in range(4):
            there = hbuf.at[x, source, block]
            pltpu.make_async_copy(there, there, a_recv.at[source, block]).wait()
        for way in range(2):
            beside_copy(x, source, way, 0).start()

    def beside_wait(source, way, hop):
        column = x + (hop + 1) * (2 * way - 1)
        there = hbuf.at[lax.rem(column + NX, NX), source]
        pltpu.make_async_copy(there, there, b_recv.at[hop, way, source]).wait()

    def pass_opposite(half):
        for way in range(2):
            source = way * 2 + half
            beside_wait(source, way, 0)
            beside_copy(x + 2 * way - 1, source, way, 1).start()

    def product(owner, piece):
        total = None
        for way in range(2):
            for distance in range(way, REACH[way] + 1):
                origin_z = lax.rem(z + (2 * way - 1) * distance + NZ, NZ)
                column, block = lax.div(origin_z, 4), lax.rem(origin_z, 4)
                rows = jnp.concatenate(
                    [hbuf[column, owner * 2 + half, block] for half in range(2)], axis=0
                )
                term = jnp.dot(
                    rows, wbuf[way, distance, piece], preferred_element_type=jnp.float32
                )
                total = term if total is None else total + term
        return total

    def to_core(piece):
        return remote(
            sums.at[piece, 0], core_in.at[piece], s_send.at[piece, 0], s_recv.at[piece, 0], sibling
        )

    def to_pair(piece):
        return remote(
            sums.at[piece, 1], pair_in.at[piece], s_send.at[piece, 1], s_recv.at[piece, 1], partner
        )

    def add_core(piece):
        to_core(piece).wait_recv()
        sums[piece, 1] = sums[piece, 1] + core_in[piece]
        to_pair(piece).start()

    def add_pair(piece):
        to_pair(piece).wait_recv()
        total = sums[piece, 1] + pair_in[piece]
        if piece == 0:
            total = total * turn[0] + pltpu.roll(total, HEAD // 2, 1) * turn[1]
        kv[core, z, piece] = total.astype(jnp.bfloat16).reshape(2, SLAB, HEAD)
        ring_go(0, piece)

    def source_z(distance, way):
        return lax.rem(z + (2 * way - 1) * distance + NZ, NZ)

    def ring_copy(distance, way, piece):
        near = TREE[distance]
        there = kv.at[core, source_z(near, way), piece]
        return remote(
            there,
            there,
            g_send.at[way, distance, piece],
            g_recv.at[way, distance, piece],
            along((distance - near) * (1 - 2 * way)),
        )

    def across_copy(distance, way, piece):
        there = kv.at[core, source_z(distance, way), piece]
        return remote(
            there,
            there,
            d_send.at[way, distance, piece],
            d_recv.at[way, distance, piece],
            sibling,
        )

    def ring_go(distance, piece):
        for way in range(2):
            if distance > REACH[way]:
                continue
            if distance:
                there = kv.at[core, source_z(distance, way), piece]
                pltpu.make_async_copy(there, there, g_recv.at[way, distance, piece]).wait()
            for far in children(distance, way):
                ring_copy(far, way, piece).start()

    def across_go(distance, piece):
        for way in range(2):
            if way <= distance <= REACH[way]:
                across_copy(distance, way, piece).start()

    factor = math.log2(math.e) / math.sqrt(HEAD)
    rows = q_ref.shape[1]

    def climb(unused, carried):
        current, path = carried
        return parent_ref[current], path | (1 << current)

    unused, path = lax.fori_loop(0, NODES, climb, (leaf_ref[0], jnp.int32(0)))

    def heads(body):
        def some(step, unused):
            for number in range(TOGETHER):
                body(step * TOGETHER + number)
            return 0

        lax.fori_loop(0, GROUP // TOGETHER, some, 0)

    def against(head, key_block):
        return lax.dot_general(
            q_ref[head], key_block, (((1,), (1,)), ((), ())), preferred_element_type=jnp.float32
        )

    def fold(score):
        most = score[:, :HEAD]
        for start in range(HEAD, score.shape[1], HEAD):
            most = jnp.maximum(most, score[:, start : start + HEAD])
        return most

    def weigh(score, most, value_block):
        wide = jnp.concatenate([most] * (score.shape[1] // HEAD), axis=1)
        weights = jnp.exp2(score * factor - wide).astype(jnp.bfloat16)
        wider = jnp.concatenate([value_block, jnp.ones_like(value_block)], axis=1)
        return jnp.dot(weights, wider, preferred_element_type=jnp.float32)

    def block_of(owner, places, piece):
        return jnp.concatenate(
            [kv[owner, source_z(d, way), piece].reshape(2 * SLAB, HEAD) for way, d in places], axis=0
        )

    def score_block(number, owner, places):
        width = len(places) * 2 * SLAB
        position = lax.broadcasted_iota(jnp.int32, (1, width), 1)
        limit = jnp.zeros((1, width), jnp.int32)
        for place_number, (way, d) in enumerate(places):
            for half in range(2):
                slab = (half * NZ + source_z(d, way)) * 2 + owner
                live = ((path >> node_ref[slab]) & 1) * len_ref[slab]
                start = (2 * place_number + half) * SLAB
                limit = jnp.where(position >= start, start + live, limit)
        bias = jnp.where(position < limit, 0.0, masked_score)
        key_block = block_of(owner, places, 0)

        def body(head):
            score = against(head, key_block) + bias
            scores[number, head, :, :width] = score
            most = fold(score)
            largest[head] = jnp.maximum(largest[head], most) if number else most

        heads(body)

    def raise_top():
        def body(head):
            most = jnp.max(largest[head], axis=1, keepdims=True) * factor
            before = top[head]
            after = jnp.maximum(before, most)
            top[head] = after
            shrink = jnp.exp2(before - after)
            mixed[head] = mixed[head] * jnp.concatenate([shrink, shrink], axis=1)

        heads(body)

    def weigh_block(number, owner, places):
        width = len(places) * 2 * SLAB
        value_block = block_of(owner, places, 1)

        def body(head):
            mixed[head] += weigh(scores[number, head, :, :width], top[head], value_block)

        heads(body)

    def attend_suffix():
        for copy in large:
            copy.wait()
        query_pos = lax.broadcasted_iota(jnp.int32, (rows, rows), 0)
        key_pos = lax.broadcasted_iota(jnp.int32, (rows, rows), 1)
        mask = (key_pos <= query_pos) & (key_pos < suffix_len_ref[0])
        key_block, value_block = sk_ref[...], sv_ref[...]

        def body(head):
            score = jnp.where(mask, against(head, key_block), masked_score)
            most = jnp.max(score, axis=1, keepdims=True) * factor
            top[head] = jnp.broadcast_to(most, (rows, HEAD))
            mixed[head] = weigh(score, top[head], value_block)

        heads(body)

    def across_wait(places):
        for way, d in places:
            for piece in range(2):
                there = kv.at[1 - core, source_z(d, way), piece]
                pltpu.make_async_copy(there, there, d_recv.at[way, d, piece]).wait()

    def attend_places(places):
        score_block(0, core, places)
        across_wait(places)
        score_block(1, 1 - core, places)
        raise_top()
        weigh_block(0, core, places)
        weigh_block(1, 1 - core, places)

    first, second = y_lo, 1 - y_lo
    weight_go(2)
    pass_on(first)
    pass_on(2 + first)
    weight_go(1)
    weight_go(4)
    pass_on(second)
    pass_on(2 + second)
    weight_go(3)
    pass_opposite(first)
    attend_suffix()
    weight_go(6)
    weight_go(5)
    pass_opposite(second)
    for half in (first, second):
        for way in range(2):
            beside_wait((1 - way) * 2 + half, way, 0)
    weight_go(8)
    weight_go(7)
    for half in (first, second):
        for way in range(2):
            beside_wait(way * 2 + half, way, 1)
    for piece in range(2):
        sums[piece, 0] = product(1 - core, piece)
        to_core(piece).start()
    for piece in range(2):
        sums[piece, 1] = product(core, piece)
    add_core(0)
    add_core(1)
    add_pair(0)
    add_pair(1)
    across_go(0, 0)
    across_go(0, 1)
    attend_places(((0, 0),))
    for stage in range(1, 5):
        for distance in (2 * stage, 2 * stage - 1):
            for piece in range(2):
                ring_go(distance, piece)
            for piece in range(2):
                across_go(distance, piece)
        attend_places(
            [
                (way, distance)
                for way in range(2)
                for distance in (2 * stage - 1, 2 * stage)
                if distance <= REACH[way]
            ]
        )
    for head in range(GROUP):
        result = mixed[head, :, :HEAD] / mixed[head, :, HEAD:]
        out_ref[:, head * HEAD : (head + 1) * HEAD] = result.astype(jnp.bfloat16)

    for way in range(2):
        for distance in range(way, REACH[way] + 1):
            for piece in range(2):
                across_copy(distance, way, piece).wait_send()
                if distance:
                    ring_copy(distance, way, piece).wait_send()
                    weight_copy(distance, way, piece).wait_send()
        for source in range(4):
            beside_copy(x, source, way, 0).wait_send()
        for half in range(2):
            beside_copy(x, way * 2 + half, way, 1).wait_send()
    for other_y in range(2):
        for other_core in range(2):
            own, copies = hidden_copies(other_y, other_core)

            @pl.when(jnp.logical_not(own))
            def _():
                for far, *unused in copies:
                    far.wait_send()

    for piece in range(2):
        to_core(piece).wait_send()
        to_pair(piece).wait_send()


def attend(hid, key_w, value_w, q, sk, sv, slab_node, slab_len, parent, leaf, suffix_len):
    freqs = rope_base ** (-2.0 * np.arange(HEAD // 2, dtype=np.float64) / HEAD)
    freqs = jnp.asarray(np.tile(freqs, 2)[None, :].astype(np.float32))
    dma = pltpu.SemaphoreType.DMA
    hbm = pl.BlockSpec(memory_space=pltpu.HBM)
    vmem = pl.BlockSpec(memory_space=pltpu.VMEM)
    rows = q.shape[0]
    smem = pl.BlockSpec(memory_space=pltpu.SMEM)

    def stay(*arrays):
        return [pltpu.with_memory_space_constraint(array, pltpu.HBM) for array in arrays]

    operands = [
        *stay(hid, key_w, value_w, slab_node, slab_len, parent),
        leaf,
        suffix_len,
        *stay(freqs, q, sk, sv),
    ]
    return pl.pallas_call(
        tree_kernel,
        out_shape=jax.ShapeDtypeStruct(q.shape, jnp.bfloat16),
        in_specs=[hbm] * 6 + [smem] * 2 + [hbm] * 4,
        out_specs=vmem,
        scratch_shapes=[
            pltpu.VMEM((2, NZ, 2, 2, SLAB, HEAD), jnp.bfloat16),
            pltpu.VMEM((GROUP, rows, HEAD), jnp.bfloat16),
            pltpu.VMEM((rows, HEAD), jnp.bfloat16),
            pltpu.VMEM((rows, HEAD), jnp.bfloat16),
            pltpu.VMEM((2, GROUP, rows, 8 * SLAB), jnp.float32),
            pltpu.VMEM((GROUP, rows, HEAD), jnp.float32),
            pltpu.VMEM((GROUP, rows, HEAD), jnp.float32),
            pltpu.VMEM((GROUP, rows, 2 * HEAD), jnp.float32),
            pltpu.VMEM((NX, 4, 4, SLAB, 128), jnp.bfloat16),
            pltpu.VMEM((2, 9, 2, 128, 128), jnp.bfloat16),
            pltpu.VMEM((2, 2, 2 * SLAB, HEAD), jnp.float32),
            pltpu.VMEM((2, 2 * SLAB, HEAD), jnp.float32),
            pltpu.VMEM((2, 2 * SLAB, HEAD), jnp.float32),
            pltpu.VMEM((2, 2 * SLAB, HEAD), jnp.float32),
            pltpu.VMEM((1, HEAD), jnp.float32),
            pltpu.SMEM((SLABS,), jnp.int32),
            pltpu.SMEM((SLABS,), jnp.int32),
            pltpu.SMEM((NODES,), jnp.int32),
            dma((6,)),
            dma((GROUP + 2,)),
            dma((2, 2, 4)),
            dma((4, 4)),
            dma((2, 2, 4)),
            dma((2, 2, 4)),
            dma((2, 9, 2)),
            dma((2, 9, 2)),
            dma((2, 2)),
            dma((2, 2)),
            dma((2, 9, 2)),
            dma((2, 9, 2)),
            dma((2, 9, 2)),
            dma((2, 9, 2)),
        ],
        compiler_params=pltpu.CompilerParams(
            collective_id=0, has_side_effects=True, vmem_limit_bytes=48 << 20
        ),
        cost_estimate=pl.CostEstimate(
            flops=5_000_000_000, bytes_accessed=4_000_000, transcendentals=9_000_000
        ),
        name="attend_tree",
    )(*operands)


def local(
    prefix_hidden,
    key_weight,
    value_weight,
    suffix_q,
    suffix_k,
    suffix_v,
    slab_node,
    slab_len,
    parent,
    leaf,
    suffix_len,
):
    return attend(
        prefix_hidden,
        key_weight,
        value_weight,
        suffix_q,
        suffix_k,
        suffix_v,
        slab_node,
        slab_len,
        parent,
        leaf,
        suffix_len,
    )


def solution(mesh):
    return jax.shard_map(
        local,
        mesh=mesh,
        in_specs=(
            P("branch", "tensor"),
            P("branch", "tensor"),
            P("branch", "tensor"),
            P("branch", "tensor"),
            P("branch", "tensor"),
            P("branch", "tensor"),
            P(),
            P(),
            P(),
            P("branch"),
            P("branch"),
        ),
        out_specs=P("branch", "tensor"),
        check_vma=False,
    )
```
